128 devices in a mesh: space: 16 (over z, x), sub: 8 (over y, core).
Axes of the slice: x: 4, y: 4, z: 4, core: 2. Of those that a mesh axis runs over, the one named last changes fastest.
Arguments:
- coords: float32 [3, 16777216], P(None, ('space', 'sub')), may hold values from -1 to 1
- masses: float32 [16777216], P(('space', 'sub')), may hold values from 0.1 to 2
- swap_counts: int32 [128, 3], P(('space', 'sub')), may hold values from 1 to 16384, as said below
- leaf_of_block: int32 [131072], P(('space', 'sub')), may hold values from 0 to 639
- let_send: int32 [128, 128, 32], P(('space', 'sub')), may hold values from 0 to 639
- inter_source: int32 [81920, 189], P(('space', 'sub')), may hold values from 0 to 4735
- inter_offset: int32 [81920, 189], P(('space', 'sub')), may hold values from 0 to 315, as said below
- compress: float32 [216, 64], replicated, may hold values from -0.4375 to 0.4375
- m2l_kernels: bfloat16 [64, 20224], replicated, may hold values from -0.0546875 to 0.0546875
- expand: float32 [64, 216], replicated, may hold values from -0.75 to 0.75
Outputs:
- potential: float32 [16777216], P(('space', 'sub'))
The draws below stay inside these ranges and needn't reach their ends.
Inputs may be any that keep to these rules, and one draw needn't show every extreme that they name: swap_counts[d, r] equals swap_counts[d XOR k_r, r] of its partner in round r. `inter_offset`: within a row, the 189 offsets are different.
All inputs are finite; a program needn't handle non-finite values.
Results may differ from the reference program's by a relative error of at most 0.003.
Values may be sent and summed in bfloat16 or wider, within the bound.
A program may use at most 192 MiB of HBM per device.

```python
import math
import jax
import jax.numpy as jnp
from jax import lax

BODY_DEV = 131072
LEAVES = 640
SEND = 32
ORDER = 6
RANK = 64
NOFF = 316
INTER = 189
NODES = 216
SWAP_MAX = 16384
SPACES = 16
SUBS = 8
BODIES = 16777216
BLOCKS = 131072
CELLS = 81920
TABLE = 4736


def draw_swap_counts(key, part):
    key = jax.random.fold_in(key, 11)
    devices = SPACES * SUBS
    raw = jax.random.randint(key, (devices, 3), 1, SWAP_MAX + 1).astype(jnp.int32)
    raw = raw.at[0].set(SWAP_MAX)
    ids = jnp.arange(devices, dtype=jnp.int32)
    masks = [SPACES // 2 * SUBS, SUBS, 1]
    columns = [jnp.maximum(raw[:, rnd], raw[jnp.bitwise_xor(ids, masks[rnd]), rnd]) for rnd in range(3)]
    return jnp.stack(columns, axis=1).astype(jnp.int32)


def draw_inter_offset(key, part):
    key = jax.random.fold_in(key, 12)
    keys = jax.random.split(key, CELLS)
    rows = jax.vmap(lambda single: jax.random.permutation(single, NOFF)[:INTER])(keys)
    return rows.astype(jnp.int32)


def touch_ends(values, rng, least, largest):
    extent = values.shape
    index_at = [jax.random.randint(jax.random.fold_in(rng, axis), (), 0, extent[axis]) for axis in range(len(extent))]
    values = values.at[tuple(index_at)].set(least)
    longest = extent.index(max(extent))
    index_at[longest] = (index_at[longest] + 1) % extent[longest]
    return values.at[tuple(index_at)].set(largest)


def block_levels(rng, extent, shards, smallest, top_value):
    level = 1.0
    for position, shards_of in shards:
        draws = jax.random.uniform(jax.random.fold_in(jax.random.fold_in(rng, 6), position), (shards_of,), jnp.float32, smallest / len(shards), top_value / len(shards))
        level = level * jnp.repeat(jnp.exp(draws), extent[position] // shards_of).reshape((-1,) + (1,) * (len(extent) - 1 - position))
    return level


def scatter_about(own_key, extent, scale, most, kind=jnp.bfloat16):
    return jnp.clip(scale * jax.random.normal(own_key, extent, jnp.float32), -most, most).astype(kind)


def setup_inputs(seed: int = 0) -> dict:
    arg_keys = jax.random.split(jax.random.key(seed), 11)
    coords = jnp.clip(jax.random.uniform(arg_keys[0], (3, BODIES), jnp.float32, -1.0, 1.0) * block_levels(arg_keys[0], (3, BODIES), ((1, 128),), -0.4, 0.0), -1.0, 1.0)
    masses = jnp.clip(jnp.exp(math.log(2.0) - 2.9957323 * jax.random.uniform(arg_keys[1], (BODIES,), jnp.float32) ** block_levels(arg_keys[1], (BODIES,), ((0, 128),), -0.2, 0.2)), 0.1, 2.0)
    swap_counts = draw_swap_counts(jax.random.fold_in(arg_keys[10], 71), 0)
    leaf_of_block = touch_ends(jax.random.randint(arg_keys[3], (BLOCKS,), 0, LEAVES), jax.random.fold_in(arg_keys[3], 1), 0, LEAVES - 1).astype(jnp.int32)
    let_send = touch_ends(jax.random.randint(arg_keys[4], (SPACES * SUBS, SPACES * SUBS, SEND), 0, LEAVES), jax.random.fold_in(arg_keys[4], 1), 0, LEAVES - 1).astype(jnp.int32)
    inter_source = touch_ends(jax.random.randint(arg_keys[5], (CELLS, INTER), 0, TABLE), jax.random.fold_in(arg_keys[5], 1), 0, TABLE - 1).astype(jnp.int32)
    inter_offset = draw_inter_offset(jax.random.fold_in(arg_keys[10], 71), 0)
    compress = scatter_about(arg_keys[7], (NODES, RANK), NODES ** -0.5, 0.4375, jnp.float32)
    m2l_kernels = scatter_about(arg_keys[8], (RANK, NOFF * RANK), (INTER * RANK) ** -0.5, 0.0546875)
    expand = scatter_about(arg_keys[9], (RANK, NODES), RANK ** -0.5, 0.75, jnp.float32)
    return {"coords": coords, "masses": masses, "swap_counts": swap_counts, "leaf_of_block": leaf_of_block, "let_send": let_send, "inter_source": inter_source, "inter_offset": inter_offset, "compress": compress, "m2l_kernels": m2l_kernels, "expand": expand}


def cheb_weights(points, order):
    nodes = jnp.cos((2.0 * jnp.arange(order, dtype=jnp.float32) + 1.0) * jnp.pi / (2.0 * order))
    shape_tail = (1,) * points.ndim
    node_prev = jnp.ones((order,), jnp.float32)
    node_cur = nodes
    poly_prev = jnp.ones_like(points)
    poly_cur = points
    total = jnp.full((order,) + points.shape, 1.0 / order, jnp.float32)
    for step in range(1, order):
        total = total + (2.0 / order) * node_cur.reshape((order,) + shape_tail) * poly_cur[None]
        node_prev, node_cur = node_cur, 2.0 * nodes * node_cur - node_prev
        poly_prev, poly_cur = poly_cur, 2.0 * points * poly_cur - poly_prev
    return total


def block_onehot(leaf, leaves):
    return (leaf[None, :] == jnp.arange(leaves, dtype=jnp.int32)[:, None]).astype(jnp.float32)


def multipoles(stacked, leaf):
    order = ORDER
    weights = cheb_weights(stacked[:3], order)
    blocks = stacked.shape[1] // 128
    pair = (weights[:, 0][:, None, :] * stacked[3][None, None, :]) * weights[:, 1][None, :, :]
    pair = pair.reshape(order * order, blocks, 128)
    per_block = jnp.einsum("pnb,knb->npk", pair, weights[:, 2].reshape(order, blocks, 128), precision=lax.Precision.HIGHEST)
    per_block = per_block.reshape(blocks, order ** 3)
    return jnp.dot(block_onehot(leaf, LEAVES), per_block, precision=lax.Precision.HIGHEST, preferred_element_type=jnp.float32)


def evaluate(stacked, leaf, local_nodes):
    order = ORDER
    weights = cheb_weights(stacked[:3], order)
    blocks = stacked.shape[1] // 128
    per_block = jnp.dot(block_onehot(leaf, LEAVES).T, local_nodes, precision=lax.Precision.HIGHEST, preferred_element_type=jnp.float32)
    per_block = per_block.reshape(blocks, order * order, order)
    pair = (weights[:, 0][:, None, :] * weights[:, 1][None, :, :]).reshape(order * order, blocks, 128)
    values = jnp.einsum("pnb,npk,knb->nb", pair, per_block, weights[:, 2].reshape(order, blocks, 128), precision=lax.Precision.HIGHEST)
    return values.reshape(-1)


def translate(table, sources, offsets, m2l_kernels, expand):
    gathered = table[sources].astype(jnp.float32)
    rows = jnp.arange(LEAVES, dtype=jnp.int32)[:, None]
    placed = jnp.zeros((LEAVES, NOFF, RANK), jnp.float32).at[rows, offsets].set(gathered)
    compressed_local = jnp.dot(placed.reshape(LEAVES, NOFF * RANK), m2l_kernels.astype(jnp.float32).T, precision=lax.Precision.HIGHEST, preferred_element_type=jnp.float32)
    return jnp.dot(compressed_local, expand, precision=lax.Precision.HIGHEST, preferred_element_type=jnp.float32)


def reference(coords, masses, swap_counts, leaf_of_block, let_send, inter_source, inter_offset, compress, m2l_kernels, expand):
    devices = SPACES * SUBS
    stacked = jnp.concatenate([coords, masses[None, :]], axis=0)
    stacked = stacked.reshape(4, devices, BODY_DEV).transpose(1, 0, 2)
    ids = jnp.arange(devices, dtype=jnp.int32)
    masks = [(SPACES // 2) * SUBS, SUBS, 1]
    columns = jnp.arange(SWAP_MAX, dtype=jnp.int32)
    for rnd in range(3):
        partner = jnp.bitwise_xor(ids, masks[rnd])
        region = stacked[:, :, rnd * SWAP_MAX:(rnd + 1) * SWAP_MAX]
        keep = columns[None, None, :] < swap_counts[:, rnd][:, None, None]
        region = jnp.where(keep, region[partner], region)
        stacked = stacked.at[:, :, rnd * SWAP_MAX:(rnd + 1) * SWAP_MAX].set(region)
    leaves = leaf_of_block.reshape(devices, BODY_DEV // 128)
    multipole = lax.map(lambda pair: multipoles(pair[0], pair[1]), (stacked, leaves))
    coeffs = jnp.dot(multipole.reshape(-1, NODES), compress, precision=lax.Precision.HIGHEST, preferred_element_type=jnp.float32)
    coeffs = coeffs.astype(jnp.bfloat16).reshape(devices, LEAVES, RANK)
    ghosts = coeffs[ids[:, None, None], let_send]
    ghosts = ghosts.transpose(1, 0, 2, 3).reshape(devices, devices * SEND, RANK)
    table = jnp.concatenate([coeffs, ghosts], axis=1)
    local_nodes = lax.map(lambda pack: translate(pack[0], pack[1], pack[2], m2l_kernels, expand),
                          (table, inter_source.reshape(devices, LEAVES, INTER), inter_offset.reshape(devices, LEAVES, INTER)))
    values = lax.map(lambda pack: evaluate(pack[0], pack[1], pack[2]), (stacked, leaves, local_nodes))
    return values.reshape(-1)
```

```python
import functools

import jax
import jax.numpy as jnp
import numpy as np
from jax import lax
from jax.experimental import pallas as pl
from jax.experimental.pallas import tpu as pltpu
from jax.sharding import PartitionSpec as P

ORDER = 6
RANK = 64
BLOCK = 128
REGION = 128
SWAPS = 3
GROUP = 80
SLOTS = 192
PAIRS = 160
PITCH = 81
UNROLL = 4


def params(**more):
    return pltpu.CompilerParams(vmem_limit_bytes=56 << 20, **more)


def from_partner(block, axis, distance):
    count = lax.axis_size(axis)
    route = []
    for low in range(count):
        high = low | 1 << distance
        if high != low and high < count:
            route += [(low, high), (high, low)]
    return lax.ppermute(block, axis, route)


def node_weights(points):
    twice = 2.0 * points
    polys = [None, points, twice * points - 1.0]
    for _ in range(3):
        polys.append(twice * polys[-1] - polys[-2])
    weights = [None] * ORDER
    for j in range(ORDER // 2):
        c = [np.float32(np.cos(k * (2 * j + 1) * np.pi / (2 * ORDER)) / 3.0) for k in range(ORDER)]
        even = np.float32(1.0 / ORDER) + c[2] * polys[2] + c[4] * polys[4]
        odd = c[1] * polys[1] + c[3] * polys[3] + c[5] * polys[5]
        weights[j] = even + odd
        weights[ORDER - 1 - j] = even - odd
    return weights


def split_three(values):
    first = values.astype(jnp.bfloat16)
    rest = values - first.astype(jnp.float32)
    second = rest.astype(jnp.bfloat16)
    third = (rest - second.astype(jnp.float32)).astype(jnp.bfloat16)
    return first, second, third


def gather_moments(bodies, out_ref, wx, wy, wz):
    mass = bodies[3].T
    for j, weight in enumerate(node_weights(bodies[0].T)):
        wx[j] = weight * mass
    for scratch, dim in ((wy, 1), (wz, 2)):
        for j, weight in enumerate(node_weights(bodies[dim].T)):
            scratch[j] = weight

    def along(i, carry):
        def chunk(v, sums):
            at = pl.ds(pl.multiple_of(v * 8, 8), 8)
            left = wx[i, at, :]
            inner = [wz[k, at, :] for k in range(ORDER)]
            new = []
            for j in range(ORDER):
                pair = left * wy[j, at, :]
                for k in range(ORDER):
                    new.append(sums[j * ORDER + k] + pair * inner[k])
            return tuple(new)

        zero = jnp.zeros((8, REGION), jnp.float32)
        sums = lax.fori_loop(0, BLOCK // 8, chunk, (zero,) * (ORDER * ORDER), unroll=4)
        for n in range(ORDER * ORDER):
            out_ref[pl.ds(i * ORDER * ORDER + n, 1), :] = jnp.sum(sums[n], axis=0, keepdims=True)
        return carry

    lax.fori_loop(0, ORDER, along, 0)


def moments_kernel(bodies_ref, out_ref, wx, wy, wz):
    gather_moments(bodies_ref, out_ref, wx, wy, wz)


def swapped_moments_kernel(counts_ref, bodies_ref, got0_ref, got1_ref, got2_ref, out_ref, merged_ref, wx, wy, wz):
    column = lax.broadcasted_iota(jnp.int32, (REGION, BLOCK), 0) * BLOCK + lax.broadcasted_iota(
        jnp.int32, (REGION, BLOCK), 1
    )
    for rnd, got in enumerate((got0_ref, got1_ref, got2_ref)):

        @pl.when(pl.program_id(0) == rnd)
        def _():
            keep = column < counts_ref[rnd]
            for dim in range(4):
                merged_ref[dim] = jnp.where(keep, got[dim], bodies_ref[dim])

    gather_moments(merged_ref, out_ref, wx, wy, wz)


def weight_scratch():
    return [pltpu.VMEM((ORDER, BLOCK, REGION), jnp.float32) for _ in range(3)]


def coefficients_kernel(send_ref, swapped_ref, stayed_ref, leaf_ref, compress_ref, own_ref, out_ref, padded):
    leaves = own_ref.shape[0]
    peers = out_ref.shape[0] // 16
    total = jnp.zeros((leaves, 2 * RANK), jnp.float32)
    at = 0
    for sums in (swapped_ref, stayed_ref):
        count = sums.shape[1]
        ids = leaf_ref[:, pl.ds(at, count)]
        onehot = lax.broadcasted_iota(jnp.int32, (leaves, count), 0) == ids
        onehot = jnp.where(onehot, 1.0, 0.0).astype(jnp.bfloat16)
        moved = jnp.dot(
            compress_ref[...], sums[...], precision=lax.Precision.HIGHEST, preferred_element_type=jnp.float32
        )
        for part in split_three(moved):
            total += lax.dot_general(onehot, part, (((1,), (1,)), ((), ())), preferred_element_type=jnp.float32)
        at += count
    own = total.astype(jnp.bfloat16).astype(jnp.float32)
    own_ref[...] = own
    padded[pl.ds(0, 8), :] = jnp.zeros((8, 2 * RANK), jnp.float32)
    padded[pl.ds(8, leaves), :] = own
    padded[pl.ds(8 + leaves, 8), :] = jnp.zeros((8, 2 * RANK), jnp.float32)
    row_of = lax.broadcasted_iota(jnp.int32, (8, 2 * RANK), 0)
    low = lax.broadcasted_iota(jnp.int32, (8, 2 * RANK), 1) < RANK

    def pack(peer, carry):
        line = send_ref.at[pl.ds(peer * 32, 32)]
        halves = []
        for start in (0, 8):
            rows = None
            for j in range(8):
                slot = 2 * (start + j)
                both = jnp.where(low, padded[pl.ds(line[slot], 8), :], padded[pl.ds(line[slot + 1], 8), :])
                rows = both if rows is None else jnp.where(row_of == j, both, rows)
            halves.append(rows)
        out_ref[pl.ds(pl.multiple_of(peer * 16, 16), 16), :] = jnp.concatenate(halves, axis=0).astype(jnp.bfloat16)
        return carry

    lax.fori_loop(0, peers, pack, 0, unroll=4)


def translate_kernel(leaves, inter, src_ref, off_ref, own_ref, ghost_ref, kernels_ref, out_ref, tab, iota, held, placed, m2l_ref, sem):
    step = pl.program_id(0)
    last = pl.num_programs(0) - 1
    rows = (tab.shape[0] - 16) // 2
    ghosts = ghost_ref.shape[0]

    @pl.when(step == 0)
    def _():
        width = kernels_ref.shape[1]
        copy = pltpu.make_async_copy(kernels_ref, m2l_ref.at[:, pl.ds(0, width)], sem)
        copy.start()
        m2l_ref[:, pl.ds(width, m2l_ref.shape[1] - width)] = jnp.zeros(
            (m2l_ref.shape[0], m2l_ref.shape[1] - width), jnp.bfloat16
        )
        iota[...] = lax.broadcasted_iota(jnp.int32, iota.shape, 0).astype(jnp.float32).astype(jnp.bfloat16)
        held[...] = jnp.zeros_like(held)
        tab[pl.ds(0, 8), :] = jnp.zeros((8, 128), jnp.float32)
        tab[pl.ds(2 * rows + 8, 8), :] = jnp.zeros((8, 128), jnp.float32)
        low = lax.broadcasted_iota(jnp.int32, (leaves, 128), 1) < 64
        own = own_ref[...]
        tab[pl.ds(8, leaves), :] = jnp.where(low, own, 0.0)
        tab[pl.ds(8 + rows, leaves), :] = jnp.where(low, 0.0, own)
        low = lax.broadcasted_iota(jnp.int32, (ghosts, 128), 1) < 64
        got = ghost_ref[...].astype(jnp.float32)
        turned = pltpu.roll(got, 64, 1)
        tab[pl.ds(8 + leaves, ghosts), :] = jnp.where(low, got, 0.0)
        tab[pl.ds(8 + leaves + ghosts, ghosts), :] = jnp.where(low, turned, 0.0)
        tab[pl.ds(8 + rows + leaves, ghosts), :] = jnp.where(low, 0.0, turned)
        tab[pl.ds(8 + rows + leaves + ghosts, ghosts), :] = jnp.where(low, 0.0, got)
        copy.wait()

    now = lax.rem(step, 2) * (PAIRS * PITCH)
    before = lax.rem(step + 1, 2) * (PAIRS * PITCH)
    lane_of = lax.broadcasted_iota(jnp.int32, (8, 128), 0)

    def collect(cells, slots):
        lines = [src_ref.at[pl.ds(cell * SLOTS, SLOTS)] for cell in cells]
        for pack in range(SLOTS // 16):
            parts = [[] for _ in cells]
            for start in (pack * 16, pack * 16 + 8):
                totals = [None] * len(cells)
                for j in range(min(8, inter - start)):
                    for u, line in enumerate(lines):
                        window = tab[pl.ds(line[start + j], 8), :]
                        totals[u] = window if j == 0 else jnp.where(lane_of == j, window, totals[u])
                for u in range(len(cells)):
                    parts[u].append(totals[u])
            for u, slot in enumerate(slots):
                held[slot, pl.ds(pack * 16, 16), :] = jnp.concatenate(parts[u], axis=0).astype(jnp.bfloat16)

    def pick(cell, rows_of):
        line = jnp.broadcast_to(off_ref[pl.ds(cell, 1), :], (16, 256)).astype(jnp.bfloat16)
        line = jnp.concatenate([line] * (PAIRS // 16), axis=0)
        chosen = jnp.where(iota[...] == line, jnp.bfloat16(1), jnp.bfloat16(0))
        return jnp.dot(chosen, rows_of, preferred_element_type=jnp.float32)

    def contract(tile, count):
        pieces = []
        for t in range(2 * count):
            at = before + (2 * tile + t) * PITCH
            pieces.append(placed[pl.ds(at, GROUP), :].astype(jnp.bfloat16))
        both = jnp.concatenate(pieces, axis=1)
        kern = m2l_ref[:, pl.ds(pl.multiple_of(tile * 256, 256), 256 * count)]
        return lax.dot_general(both, kern, (((1,), (1,)), ((), ())), preferred_element_type=jnp.float32)

    out_ref[...] = jnp.zeros_like(out_ref)

    @pl.when(step < last)
    def _():
        def body(it, carry):
            cell = UNROLL * it
            mine = lax.rem(it, 2) * UNROLL
            other = UNROLL - mine
            part = contract(cell, UNROLL)
            olds = [held[other + u] for u in range(UNROLL)]
            results = []
            for u in range(UNROLL):
                back = jnp.where(it == 0, GROUP - UNROLL + u, cell - UNROLL + u)
                results.append((back, pick(back, olds[u])))
            collect([cell + u for u in range(UNROLL)], [mine + u for u in range(UNROLL)])
            for back, result in results:
                placed[pl.ds(now + back, PAIRS, stride=PITCH), :] = result
            out_ref[...] += part
            return carry
        lax.fori_loop(0, GROUP // UNROLL, body, 0)
        mine = (GROUP // UNROLL - 1) % 2 * UNROLL
        for u in range(UNROLL):
            back = GROUP - UNROLL + u
            placed[pl.ds(now + back, PAIRS, stride=PITCH), :] = pick(back, held[mine + u])

    @pl.when(step == last)
    def _():
        def body(it, carry):
            out_ref[...] += contract(it * UNROLL, UNROLL)
            return carry
        lax.fori_loop(0, GROUP // UNROLL, body, 0)


def translate(own, ghost, sources, offsets, m2l_kernels):
    leaves, inter = sources.shape
    ghosts = ghost.shape[0]
    rows = leaves + 2 * ghosts
    remote = sources - leaves
    row = jnp.where(remote < 0, sources, leaves + lax.shift_right_arithmetic(remote, 1) + (remote & 1) * ghosts)
    row = row + (offsets & 1) * rows
    row = row + 8 - jnp.arange(inter, dtype=jnp.int32)[None, :] % 8
    row = jnp.pad(row, ((0, 0), (0, SLOTS - inter))).reshape(-1)
    pair = jnp.pad((offsets >> 1).astype(jnp.float32), ((0, 0), (0, 256 - inter)), constant_values=-1.0)
    steps = leaves // GROUP
    return pl.pallas_call(
        functools.partial(translate_kernel, leaves, inter),
        grid=(steps + 1,),
        in_specs=[
            pl.BlockSpec((GROUP * SLOTS,), lambda i: (jnp.minimum(i, steps - 1),), memory_space=pltpu.SMEM),
            pl.BlockSpec((GROUP, 256), lambda i: (jnp.minimum(i, steps - 1), 0)),
            pl.BlockSpec(own.shape, lambda i: (0, 0)),
            pl.BlockSpec(ghost.shape, lambda i: (0, 0)),
            pl.BlockSpec(memory_space=pl.ANY),
        ],
        out_specs=pl.BlockSpec((GROUP, 64), lambda i: (jnp.maximum(i - 1, 0), 0)),
        out_shape=jax.ShapeDtypeStruct((leaves, 64), jnp.float32),
        scratch_shapes=[
            pltpu.VMEM((2 * rows + 16, 128), jnp.float32),
            pltpu.VMEM((PAIRS, 256), jnp.bfloat16),
            pltpu.VMEM((2 * UNROLL, 256, 128), jnp.bfloat16),
            pltpu.VMEM((2 * PAIRS * PITCH, 128), jnp.float32),
            pltpu.VMEM((RANK, PAIRS * 128), jnp.bfloat16),
            pltpu.SemaphoreType.DMA,
        ],
        compiler_params=params(),
    )(row, pair, own, ghost, m2l_kernels)


def evaluate_kernel(merged_ref, bodies_ref, leaf_ref, local_ref, expand_ref, out_ref, bodies, nodes0, nodes1, nodes2, nodes, result):
    step = pl.program_id(0)
    leaves = local_ref.shape[0]
    parts = (nodes0, nodes1, nodes2)

    @pl.when(step == 0)
    def _():
        full = lax.dot_general(
            expand_ref[...],
            local_ref[...],
            (((1,), (1,)), ((), ())),
            precision=lax.Precision.HIGHEST,
            preferred_element_type=jnp.float32,
        )
        for scratch, part in zip(parts, split_three(full)):
            scratch[...] = part

    @pl.when(step < SWAPS)
    def _():
        for dim in range(3):
            bodies[dim] = merged_ref[dim].T

    @pl.when(step >= SWAPS)
    def _():
        for dim in range(3):
            bodies[dim] = bodies_ref[dim].T

    onehot = lax.broadcasted_iota(jnp.int32, (leaves, REGION), 0) == leaf_ref[...]
    onehot = jnp.where(onehot, 1.0, 0.0).astype(jnp.bfloat16)
    total = jnp.dot(nodes0[...], onehot, preferred_element_type=jnp.float32)
    total += jnp.dot(nodes1[...], onehot, preferred_element_type=jnp.float32)
    total += jnp.dot(nodes2[...], onehot, preferred_element_type=jnp.float32)
    nodes[...] = total

    def chunk(v, carry):
        at = pl.ds(pl.multiple_of(v * 16, 16), 16)
        wx, wy, wz = (node_weights(bodies[dim, at, :]) for dim in range(3))
        value = None
        for i in range(ORDER):
            middle = None
            for j in range(ORDER):
                inner = None
                for k in range(ORDER):
                    term = nodes[pl.ds((i * ORDER + j) * ORDER + k, 1), :] * wz[k]
                    inner = term if inner is None else inner + term
                inner = inner * wy[j]
                middle = inner if middle is None else middle + inner
            middle = middle * wx[i]
            value = middle if value is None else value + middle
        result[at, :] = value
        return carry

    lax.fori_loop(0, BLOCK // 16, chunk, 0)
    out_ref[...] = result[...].T


def on_device(
    coords,
    masses,
    swap_counts,
    leaf_of_block,
    let_send,
    inter_source,
    inter_offset,
    compress,
    m2l_kernels,
    expand,
):
    nodes_count = compress.shape[0]
    leaves = inter_source.shape[0]
    local_bodies = coords.shape[1]
    blocks = local_bodies // BLOCK
    regions = blocks // REGION
    peers, per_peer = let_send.shape[1:]
    bodies = jnp.concatenate([coords.reshape(3, blocks, BLOCK), masses.reshape(1, blocks, BLOCK)], axis=0)
    top_bit = lax.axis_size("space").bit_length() - 2
    got_outer = from_partner(bodies[:, 0:REGION], "space", top_bit)
    got_inner = from_partner(bodies[:, REGION : 2 * REGION], "space", 0)
    got_sub = from_partner(bodies[:, 2 * REGION : 3 * REGION], "sub", 0)
    block4 = (4, REGION, BLOCK)
    stayed = pl.pallas_call(
        moments_kernel,
        grid=(regions - SWAPS,),
        in_specs=[pl.BlockSpec(block4, lambda g: (0, g + SWAPS, 0))],
        out_specs=pl.BlockSpec((nodes_count, REGION), lambda g: (0, g)),
        out_shape=jax.ShapeDtypeStruct((nodes_count, (regions - SWAPS) * REGION), jnp.float32),
        scratch_shapes=weight_scratch(),
        compiler_params=params(),
        cost_estimate=pl.CostEstimate(flops=50_000_000, bytes_accessed=4_000_000, transcendentals=0),
    )(bodies)
    whole4 = pl.BlockSpec(block4, lambda g: (0, 0, 0))
    swapped, merged = pl.pallas_call(
        swapped_moments_kernel,
        grid=(SWAPS,),
        in_specs=[
            pl.BlockSpec(memory_space=pltpu.SMEM),
            pl.BlockSpec(block4, lambda g: (0, g, 0)),
            whole4,
            whole4,
            whole4,
        ],
        out_specs=[
            pl.BlockSpec((nodes_count, REGION), lambda g: (0, g)),
            pl.BlockSpec(block4, lambda g: (0, g, 0)),
        ],
        out_shape=[
            jax.ShapeDtypeStruct((nodes_count, SWAPS * REGION), jnp.float32),
            jax.ShapeDtypeStruct((4, SWAPS * REGION, BLOCK), jnp.float32),
        ],
        scratch_shapes=weight_scratch(),
        compiler_params=params(),
    )(swap_counts.reshape(SWAPS), bodies, got_outer, got_inner, got_sub)
    leaf_row = leaf_of_block.reshape(1, blocks)
    send = let_send.reshape(peers, per_peer) + 8 - (jnp.arange(per_peer, dtype=jnp.int32)[None, :] // 2) % 8
    compress_twice = jnp.concatenate([compress.T, compress.T], axis=0)
    vmem = pl.BlockSpec(memory_space=pltpu.VMEM)
    own, outgoing = pl.pallas_call(
        coefficients_kernel,
        in_specs=[pl.BlockSpec(memory_space=pltpu.SMEM), vmem, vmem, vmem, vmem],
        out_specs=[vmem, vmem],
        out_shape=[
            jax.ShapeDtypeStruct((leaves, 2 * RANK), jnp.float32),
            jax.ShapeDtypeStruct((peers * per_peer // 2, 2 * RANK), jnp.bfloat16),
        ],
        scratch_shapes=[pltpu.VMEM((leaves + 16, 2 * RANK), jnp.float32)],
        compiler_params=params(),
    )(send.reshape(-1), swapped, stayed, leaf_row, compress_twice)
    incoming = lax.all_to_all(
        outgoing.reshape(peers, per_peer // 2, 2 * RANK), ("space", "sub"), split_axis=0, concat_axis=0, tiled=True
    )
    local = translate(own, incoming.reshape(peers * per_peer // 2, 2 * RANK), inter_source, inter_offset, m2l_kernels)
    values = pl.pallas_call(
        evaluate_kernel,
        grid=(regions,),
        in_specs=[
            pl.BlockSpec(block4, lambda g: (0, jnp.minimum(g, SWAPS - 1), 0)),
            pl.BlockSpec(block4, lambda g: (0, jnp.maximum(g, SWAPS), 0)),
            pl.BlockSpec((1, REGION), lambda g: (0, g)),
            pl.BlockSpec((leaves, RANK), lambda g: (0, 0)),
            pl.BlockSpec((nodes_count, RANK), lambda g: (0, 0)),
        ],
        out_specs=pl.BlockSpec((REGION, BLOCK), lambda g: (g, 0)),
        out_shape=jax.ShapeDtypeStruct((blocks, BLOCK), jnp.float32),
        scratch_shapes=[
            pltpu.VMEM((3, BLOCK, REGION), jnp.float32),
            pltpu.VMEM((nodes_count, leaves), jnp.bfloat16),
            pltpu.VMEM((nodes_count, leaves), jnp.bfloat16),
            pltpu.VMEM((nodes_count, leaves), jnp.bfloat16),
            pltpu.VMEM((nodes_count, REGION), jnp.float32),
            pltpu.VMEM((BLOCK, REGION), jnp.float32),
        ],
        compiler_params=params(),
    )(merged, bodies, leaf_row, local, expand.T)
    return values.reshape(local_bodies)


def solution(mesh):
    return jax.shard_map(
        on_device,
        mesh=mesh,
        in_specs=(
            P(None, ("space", "sub")),
            P(("space", "sub")),
            P(("space", "sub"), None),
            P(("space", "sub")),
            P(("space", "sub"), None, None),
            P(("space", "sub"), None),
            P(("space", "sub"), None),
            P(),
            P(),
            P(),
        ),
        out_specs=P(("space", "sub")),
        check_vma=False,
    )
```

```python
import functools

import jax
import jax.numpy as jnp
import numpy as np
from jax import lax
from jax.experimental import pallas as pl
from jax.experimental.pallas import tpu as pltpu
from jax.sharding import PartitionSpec as P

ORDER = 6
RANK = 64
BLOCK = 128
REGION = 128
SWAPS = 3
GROUP = 80
SLOTS = 192
PAIRS = 160
PITCH = 81
UNROLL = 8


def params(**more):
    return pltpu.CompilerParams(vmem_limit_bytes=56 << 20, **more)


def from_partner(block, axis, distance):
    count = lax.axis_size(axis)
    route = []
    for low in range(count):
        high = low | 1 << distance
        if high != low and high < count:
            route += [(low, high), (high, low)]
    return lax.ppermute(block, axis, route)


def chebyshev(points):
    twice = 2.0 * points
    polys = [points, twice * points - 1.0]
    for _ in range(ORDER - 3):
        polys.append(twice * polys[-1] - polys[-2])
    return polys


def node_basis():
    single = np.zeros((ORDER, ORDER))
    for j in range(ORDER):
        for k in range(ORDER):
            single[j, k] = np.cos(k * (2 * j + 1) * np.pi / (2 * ORDER)) * (1.0 if k == 0 else 2.0) / ORDER
    return np.kron(np.kron(single, single), single).astype(np.float32)


def split_two(values):
    first = values.astype(jnp.bfloat16)
    return first, (values - first.astype(jnp.float32)).astype(jnp.bfloat16)


def gather_moments(bodies, out_ref, turned_ref, px, py, pz, partial):
    mass = bodies[3].T
    px[0] = mass
    for dim, scratch in enumerate((px, py, pz)):
        points = bodies[dim].T
        turned_ref[dim] = points
        for k, poly in enumerate(chebyshev(points)):
            scratch[k + 1] = poly * mass if dim == 0 else poly

    def along(i, carry):
        def chunk(v, sums):
            at = pl.ds(pl.multiple_of(v * 8, 8), 8)
            left = px[i, at, :]
            inner = [pz[k, at, :] for k in range(1, ORDER)]
            new = []
            for j in range(ORDER):
                pair = left if j == 0 else left * py[j, at, :]
                new.append(sums[j * ORDER] + pair)
                for k in range(1, ORDER):
                    new.append(sums[j * ORDER + k] + pair * inner[k - 1])
            return tuple(new)

        zero = jnp.zeros((8, REGION), jnp.float32)
        sums = lax.fori_loop(0, BLOCK // 8, chunk, (zero,) * (ORDER * ORDER), unroll=4)
        for n in range(ORDER * ORDER):
            partial[pl.ds(pl.multiple_of((i * ORDER * ORDER + n) * 8, 8), 8), :] = sums[n]
        return carry

    lax.fori_loop(0, ORDER, along, 0)
    count = out_ref.shape[0]
    total = partial[pl.ds(0, count, stride=8), :]
    for s in range(1, 8):
        total += partial[pl.ds(s, count, stride=8), :]
    out_ref[...] = total


def moments_kernel(bodies_ref, out_ref, turned_ref, px, py, pz, partial):
    gather_moments(bodies_ref, out_ref, turned_ref, px, py, pz, partial)


def swapped_moments_kernel(
    counts_ref, bodies_ref, got0_ref, got1_ref, got2_ref, out_ref, turned_ref, merged, px, py, pz, partial
):
    column = lax.broadcasted_iota(jnp.int32, (REGION, BLOCK), 0) * BLOCK + lax.broadcasted_iota(
        jnp.int32, (REGION, BLOCK), 1
    )
    for rnd, got in enumerate((got0_ref, got1_ref, got2_ref)):

        @pl.when(pl.program_id(0) == rnd)
        def _():
            keep = column < counts_ref[rnd]
            for dim in range(4):
                merged[dim] = jnp.where(keep, got[dim], bodies_ref[dim])

    gather_moments(merged, out_ref, turned_ref, px, py, pz, partial)


def moment_scratch(nodes_count):
    return [pltpu.VMEM((ORDER, BLOCK, REGION), jnp.float32) for _ in range(3)] + [
        pltpu.VMEM((8 * nodes_count, REGION), jnp.float32)
    ]


def coefficients_kernel(send_ref, swapped_ref, stayed_ref, leaf_ref, compress_ref, own_ref, out_ref, padded):
    leaves = own_ref.shape[0]
    peers = out_ref.shape[0] // 16
    total = jnp.zeros((leaves, 2 * RANK), jnp.float32)
    at = 0
    for sums in (swapped_ref, stayed_ref):
        count = sums.shape[1]
        ids = leaf_ref[:, pl.ds(at, count)]
        onehot = lax.broadcasted_iota(jnp.int32, (leaves, count), 0) == ids
        onehot = jnp.where(onehot, 1.0, 0.0).astype(jnp.bfloat16)
        moved = jnp.dot(
            compress_ref[...], sums[...], precision=lax.Precision.HIGHEST, preferred_element_type=jnp.float32
        )
        both = jnp.concatenate(split_two(moved), axis=0)
        total += lax.dot_general(onehot, both, (((1,), (1,)), ((), ())), preferred_element_type=jnp.float32)
        at += count
    own = (total + pltpu.roll(total, RANK, 1)).astype(jnp.bfloat16).astype(jnp.float32)
    own_ref[...] = own
    padded[pl.ds(0, 8), :] = jnp.zeros((8, 2 * RANK), jnp.float32)
    padded[pl.ds(8, leaves), :] = own
    padded[pl.ds(8 + leaves, 8), :] = jnp.zeros((8, 2 * RANK), jnp.float32)
    row_of = lax.broadcasted_iota(jnp.int32, (8, 2 * RANK), 0)
    low = lax.broadcasted_iota(jnp.int32, (8, 2 * RANK), 1) < RANK

    def pack(peer, carry):
        line = send_ref.at[pl.ds(peer * 32, 32)]
        halves = []
        for start in (0, 8):
            rows = None
            for j in range(8):
                slot = 2 * (start + j)
                both = jnp.where(low, padded[pl.ds(line[slot], 8), :], padded[pl.ds(line[slot + 1], 8), :])
                rows = both if rows is None else jnp.where(row_of == j, both, rows)
            halves.append(rows)
        out_ref[pl.ds(pl.multiple_of(peer * 16, 16), 16), :] = jnp.concatenate(halves, axis=0).astype(jnp.bfloat16)
        return carry

    lax.fori_loop(0, peers, pack, 0, unroll=4)


def translate_kernel(leaves, inter, src_ref, off_ref, own_ref, ghost_ref, kernels_ref, out_ref, tab, iota, held, placed, m2l_ref, sem):
    step = pl.program_id(0)
    last = pl.num_programs(0) - 1
    rows = (tab.shape[0] - 16) // 2
    ghosts = ghost_ref.shape[0]

    @pl.when(step == 0)
    def _():
        width = kernels_ref.shape[1]
        copy = pltpu.make_async_copy(kernels_ref, m2l_ref.at[:, pl.ds(0, width)], sem)
        copy.start()
        m2l_ref[:, pl.ds(width, m2l_ref.shape[1] - width)] = jnp.zeros(
            (m2l_ref.shape[0], m2l_ref.shape[1] - width), jnp.bfloat16
        )
        iota[...] = lax.broadcasted_iota(jnp.int32, iota.shape, 0).astype(jnp.float32).astype(jnp.bfloat16)
        held[...] = jnp.zeros_like(held)
        tab[pl.ds(0, 8), :] = jnp.zeros((8, 128), jnp.float32)
        tab[pl.ds(2 * rows + 8, 8), :] = jnp.zeros((8, 128), jnp.float32)
        low = lax.broadcasted_iota(jnp.int32, (leaves, 128), 1) < 64
        own = own_ref[...]
        tab[pl.ds(8, leaves), :] = jnp.where(low, own, 0.0)
        tab[pl.ds(8 + rows, leaves), :] = jnp.where(low, 0.0, own)
        low = lax.broadcasted_iota(jnp.int32, (ghosts, 128), 1) < 64
        got = ghost_ref[...].astype(jnp.float32)
        turned = pltpu.roll(got, 64, 1)
        tab[pl.ds(8 + leaves, ghosts), :] = jnp.where(low, got, 0.0)
        tab[pl.ds(8 + leaves + ghosts, ghosts), :] = jnp.where(low, turned, 0.0)
        tab[pl.ds(8 + rows + leaves, ghosts), :] = jnp.where(low, 0.0, turned)
        tab[pl.ds(8 + rows + leaves + ghosts, ghosts), :] = jnp.where(low, 0.0, got)
        copy.wait()

    now = lax.rem(step, 2) * (PAIRS * PITCH)
    before = lax.rem(step + 1, 2) * (PAIRS * PITCH)
    lane_of = lax.broadcasted_iota(jnp.int32, (8, 128), 0)

    def collect(cells, slots):
        lines = [src_ref.at[pl.ds(cell * SLOTS, SLOTS)] for cell in cells]
        for pack in range(SLOTS // 16):
            parts = [[] for _ in cells]
            for start in (pack * 16, pack * 16 + 8):
                totals = [None] * len(cells)
                for j in range(min(8, inter - start)):
                    for u, line in enumerate(lines):
                        window = tab[pl.ds(line[start + j], 8), :]
                        totals[u] = window if j == 0 else jnp.where(lane_of == j, window, totals[u])
                for u in range(len(cells)):
                    parts[u].append(totals[u])
            for u, slot in enumerate(slots):
                held[slot, pl.ds(pack * 16, 16), :] = jnp.concatenate(parts[u], axis=0).astype(jnp.bfloat16)

    def pick(cell, rows_of):
        line = jnp.broadcast_to(off_ref[pl.ds(cell, 1), :], (16, 256)).astype(jnp.bfloat16)
        line = jnp.concatenate([line] * (PAIRS // 16), axis=0)
        chosen = jnp.where(iota[...] == line, jnp.bfloat16(1), jnp.bfloat16(0))
        return jnp.dot(chosen, rows_of, preferred_element_type=jnp.float32)

    def contract(tile, count):
        pieces = []
        for t in range(2 * count):
            at = before + (2 * tile + t) * PITCH
            pieces.append(placed[pl.ds(at, GROUP), :].astype(jnp.bfloat16))
        both = jnp.concatenate(pieces, axis=1)
        kern = m2l_ref[:, pl.ds(pl.multiple_of(tile * 256, 256), 256 * count)]
        return lax.dot_general(both, kern, (((1,), (1,)), ((), ())), preferred_element_type=jnp.float32)

    out_ref[...] = jnp.zeros_like(out_ref)

    @pl.when(step < last)
    def _():
        def body(it, carry):
            cell = UNROLL * it
            part = contract(cell, UNROLL)
            olds = [held[u] for u in range(UNROLL)]
            results = []
            for u in range(UNROLL):
                back = jnp.where(it == 0, GROUP - UNROLL, cell - UNROLL) + u
                results.append((back, pick(back, olds[u])))
            collect([cell + u for u in range(UNROLL)], list(range(UNROLL)))
            for back, result in results:
                placed[pl.ds(now + back, PAIRS, stride=PITCH), :] = result
            out_ref[...] += part
            return carry
        lax.fori_loop(0, GROUP // UNROLL, body, 0)
        for u in range(UNROLL):
            back = GROUP - UNROLL + u
            placed[pl.ds(now + back, PAIRS, stride=PITCH), :] = pick(back, held[u])

    @pl.when(step == last)
    def _():
        def body(it, carry):
            out_ref[...] += contract(it * UNROLL, UNROLL)
            return carry
        lax.fori_loop(0, GROUP // UNROLL, body, 0)


def translate(own, ghost, sources, offsets, m2l_kernels):
    leaves, inter = sources.shape
    ghosts = ghost.shape[0]
    rows = leaves + 2 * ghosts
    remote = sources - leaves
    row = jnp.where(remote < 0, sources, leaves + lax.shift_right_arithmetic(remote, 1) + (remote & 1) * ghosts)
    row = row + (offsets & 1) * rows
    row = row + 8 - jnp.arange(inter, dtype=jnp.int32)[None, :] % 8
    row = jnp.pad(row, ((0, 0), (0, SLOTS - inter))).reshape(-1)
    pair = jnp.pad((offsets >> 1).astype(jnp.float32), ((0, 0), (0, 256 - inter)), constant_values=-1.0)
    steps = leaves // GROUP
    return pl.pallas_call(
        functools.partial(translate_kernel, leaves, inter),
        grid=(steps + 1,),
        in_specs=[
            pl.BlockSpec((GROUP * SLOTS,), lambda i: (jnp.minimum(i, steps - 1),), memory_space=pltpu.SMEM),
            pl.BlockSpec((GROUP, 256), lambda i: (jnp.minimum(i, steps - 1), 0)),
            pl.BlockSpec(own.shape, lambda i: (0, 0)),
            pl.BlockSpec(ghost.shape, lambda i: (0, 0)),
            pl.BlockSpec(memory_space=pl.ANY),
        ],
        out_specs=pl.BlockSpec((GROUP, 64), lambda i: (jnp.maximum(i - 1, 0), 0)),
        out_shape=jax.ShapeDtypeStruct((leaves, 64), jnp.float32),
        scratch_shapes=[
            pltpu.VMEM((2 * rows + 16, 128), jnp.float32),
            pltpu.VMEM((PAIRS, 256), jnp.bfloat16),
            pltpu.VMEM((UNROLL, 256, 128), jnp.bfloat16),
            pltpu.VMEM((2 * PAIRS * PITCH, 128), jnp.float32),
            pltpu.VMEM((RANK, PAIRS * 128), jnp.bfloat16),
            pltpu.SemaphoreType.DMA,
        ],
        compiler_params=params(),
    )(row, pair, own, ghost, m2l_kernels)


def evaluate_kernel(swapped_ref, stayed_ref, leaf_ref, local_ref, expand_ref, out_ref, bodies, nodes, result):
    step = pl.program_id(0)
    leaves = local_ref.shape[0]
    count = expand_ref.shape[0]

    @pl.when(step == 0)
    def _():
        full = lax.dot_general(
            expand_ref[...],
            local_ref[...],
            (((1,), (1,)), ((), ())),
            precision=lax.Precision.HIGHEST,
            preferred_element_type=jnp.float32,
        )
        parts = jnp.concatenate(split_two(full), axis=0)
        for region in range(nodes.shape[0]):
            ids = leaf_ref[:, pl.ds(region * REGION, REGION)]
            onehot = lax.broadcasted_iota(jnp.int32, (leaves, REGION), 0) == ids
            onehot = jnp.where(onehot, 1.0, 0.0).astype(jnp.bfloat16)
            picked = jnp.dot(parts, onehot, preferred_element_type=jnp.float32)
            nodes[region] = picked[:count] + picked[count:]

    @pl.when(step < SWAPS)
    def _():
        bodies[...] = swapped_ref[...]

    @pl.when(step >= SWAPS)
    def _():
        bodies[...] = stayed_ref[...]

    def chunk(v, carry):
        at = pl.ds(pl.multiple_of(v * 16, 16), 16)
        px, py, pz = (chebyshev(bodies[dim, at, :]) for dim in range(3))
        value = None
        for i in range(ORDER):
            middle = None
            for j in range(ORDER):
                first = (i * ORDER + j) * ORDER
                inner = nodes[step, pl.ds(first + 1, 1), :] * pz[0] + nodes[step, pl.ds(first, 1), :]
                for k in range(2, ORDER):
                    inner += nodes[step, pl.ds(first + k, 1), :] * pz[k - 1]
                middle = inner if j == 0 else middle + inner * py[j - 1]
            value = middle if i == 0 else value + middle * px[i - 1]
        result[at, :] = value
        return carry

    lax.fori_loop(0, BLOCK // 16, chunk, 0)
    out_ref[...] = result[...].T


def on_device(
    coords,
    masses,
    swap_counts,
    leaf_of_block,
    let_send,
    inter_source,
    inter_offset,
    compress,
    m2l_kernels,
    expand,
):
    nodes_count = compress.shape[0]
    leaves = inter_source.shape[0]
    local_bodies = coords.shape[1]
    blocks = local_bodies // BLOCK
    regions = blocks // REGION
    peers, per_peer = let_send.shape[1:]
    bodies = jnp.concatenate([coords.reshape(3, blocks, BLOCK), masses.reshape(1, blocks, BLOCK)], axis=0)
    top_bit = lax.axis_size("space").bit_length() - 2
    got_outer = from_partner(bodies[:, 0:REGION], "space", top_bit)
    got_inner = from_partner(bodies[:, REGION : 2 * REGION], "space", 0)
    got_sub = from_partner(bodies[:, 2 * REGION : 3 * REGION], "sub", 0)
    block4 = (4, REGION, BLOCK)
    sums_spec = pl.BlockSpec((nodes_count, REGION), lambda g: (0, g))
    turned_spec = pl.BlockSpec((3, BLOCK, REGION), lambda g: (0, 0, g))
    stays = regions - SWAPS
    stayed, stayed_turned = pl.pallas_call(
        moments_kernel,
        grid=(stays,),
        in_specs=[pl.BlockSpec(block4, lambda g: (0, g + SWAPS, 0))],
        out_specs=[sums_spec, turned_spec],
        out_shape=[
            jax.ShapeDtypeStruct((nodes_count, stays * REGION), jnp.float32),
            jax.ShapeDtypeStruct((3, BLOCK, stays * REGION), jnp.float32),
        ],
        scratch_shapes=moment_scratch(nodes_count),
        compiler_params=params(),
        cost_estimate=pl.CostEstimate(flops=50_000_000, bytes_accessed=4_000_000, transcendentals=0),
    )(bodies)
    whole4 = pl.BlockSpec(block4, lambda g: (0, 0, 0))
    swapped, swapped_turned = pl.pallas_call(
        swapped_moments_kernel,
        grid=(SWAPS,),
        in_specs=[
            pl.BlockSpec(memory_space=pltpu.SMEM),
            pl.BlockSpec(block4, lambda g: (0, g, 0)),
            whole4,
            whole4,
            whole4,
        ],
        out_specs=[sums_spec, turned_spec],
        out_shape=[
            jax.ShapeDtypeStruct((nodes_count, SWAPS * REGION), jnp.float32),
            jax.ShapeDtypeStruct((3, BLOCK, SWAPS * REGION), jnp.float32),
        ],
        scratch_shapes=[pltpu.VMEM(block4, jnp.float32)] + moment_scratch(nodes_count),
        compiler_params=params(),
    )(swap_counts.reshape(SWAPS), bodies, got_outer, got_inner, got_sub)
    basis = node_basis()
    exact = functools.partial(jnp.dot, precision=lax.Precision.HIGHEST, preferred_element_type=jnp.float32)
    compress_polys = exact(compress.T, basis)
    expand_polys = exact(basis.T, expand.T)
    leaf_row = leaf_of_block.reshape(1, blocks)
    send = let_send.reshape(peers, per_peer) + 8 - (jnp.arange(per_peer, dtype=jnp.int32)[None, :] // 2) % 8
    vmem = pl.BlockSpec(memory_space=pltpu.VMEM)
    own, outgoing = pl.pallas_call(
        coefficients_kernel,
        in_specs=[pl.BlockSpec(memory_space=pltpu.SMEM), vmem, vmem, vmem, vmem],
        out_specs=[vmem, vmem],
        out_shape=[
            jax.ShapeDtypeStruct((leaves, 2 * RANK), jnp.float32),
            jax.ShapeDtypeStruct((peers * per_peer // 2, 2 * RANK), jnp.bfloat16),
        ],
        scratch_shapes=[pltpu.VMEM((leaves + 16, 2 * RANK), jnp.float32)],
        compiler_params=params(),
    )(send.reshape(-1), swapped, stayed, leaf_row, compress_polys)
    incoming = lax.all_to_all(
        outgoing.reshape(peers, per_peer // 2, 2 * RANK), ("space", "sub"), split_axis=0, concat_axis=0, tiled=True
    )
    local = translate(own, incoming.reshape(peers * per_peer // 2, 2 * RANK), inter_source, inter_offset, m2l_kernels)
    values = pl.pallas_call(
        evaluate_kernel,
        grid=(regions,),
        in_specs=[
            pl.BlockSpec((3, BLOCK, REGION), lambda g: (0, 0, jnp.minimum(g, SWAPS - 1))),
            pl.BlockSpec((3, BLOCK, REGION), lambda g: (0, 0, jnp.maximum(g - SWAPS, 0))),
            pl.BlockSpec((1, blocks), lambda g: (0, 0)),
            pl.BlockSpec((leaves, RANK), lambda g: (0, 0)),
            pl.BlockSpec((nodes_count, RANK), lambda g: (0, 0)),
        ],
        out_specs=pl.BlockSpec((REGION, BLOCK), lambda g: (g, 0)),
        out_shape=jax.ShapeDtypeStruct((blocks, BLOCK), jnp.float32),
        scratch_shapes=[
            pltpu.VMEM((3, BLOCK, REGION), jnp.float32),
            pltpu.VMEM((regions, nodes_count, REGION), jnp.float32),
            pltpu.VMEM((BLOCK, REGION), jnp.float32),
        ],
        compiler_params=params(),
    )(swapped_turned, stayed_turned, leaf_row, local, expand_polys)
    return values.reshape(local_bodies)


def solution(mesh):
    return jax.shard_map(
        on_device,
        mesh=mesh,
        in_specs=(
            P(None, ("space", "sub")),
            P(("space", "sub")),
            P(("space", "sub"), None),
            P(("space", "sub")),
            P(("space", "sub"), None, None),
            P(("space", "sub"), None),
            P(("space", "sub"), None),
            P(),
            P(),
            P(),
        ),
        out_specs=P(("space", "sub")),
        check_vma=False,
    )
```

```python
import functools

import jax
import jax.numpy as jnp
import numpy as np
from jax import lax
from jax.experimental import pallas as pl
from jax.experimental.pallas import tpu as pltpu
from jax.sharding import PartitionSpec as P

ORDER = 6
RANK = 64
BLOCK = 128
REGION = 128
SWAPS = 3
GROUP = 80
SLOTS = 192
PAIRS = 160
PITCH = 81
UNROLL = 8


def params(**more):
    return pltpu.CompilerParams(vmem_limit_bytes=56 << 20, **more)


def from_partner(block, axis, distance):
    count = lax.axis_size(axis)
    route = []
    for low in range(count):
        high = low | 1 << distance
        if high != low and high < count:
            route += [(low, high), (high, low)]
    return lax.ppermute(block, axis, route)


def chebyshev(points):
    twice = 2.0 * points
    polys = [points, twice * points - 1.0]
    for _ in range(ORDER - 3):
        polys.append(twice * polys[-1] - polys[-2])
    return polys


def node_basis():
    single = np.zeros((ORDER, ORDER))
    for j in range(ORDER):
        for k in range(ORDER):
            single[j, k] = np.cos(k * (2 * j + 1) * np.pi / (2 * ORDER)) * (1.0 if k == 0 else 2.0) / ORDER
    return np.kron(np.kron(single, single), single).astype(np.float32)


def split_two(values):
    first = values.astype(jnp.bfloat16)
    return first, (values - first.astype(jnp.float32)).astype(jnp.bfloat16)


def gather_moments(bodies, out_ref, turned_ref, px, py, pz, partial):
    mass = bodies[3].T
    px[0] = mass
    for dim, scratch in enumerate((px, py, pz)):
        points = bodies[dim].T
        turned_ref[dim] = points
        for k, poly in enumerate(chebyshev(points)):
            scratch[k + 1] = poly * mass if dim == 0 else poly

    def along(i, carry):
        def chunk(v, sums):
            at = pl.ds(pl.multiple_of(v * 8, 8), 8)
            left = px[i, at, :]
            inner = [pz[k, at, :] for k in range(1, ORDER)]
            new = []
            for j in range(ORDER):
                pair = left if j == 0 else left * py[j, at, :]
                new.append(sums[j * ORDER] + pair)
                for k in range(1, ORDER):
                    new.append(sums[j * ORDER + k] + pair * inner[k - 1])
            return tuple(new)

        zero = jnp.zeros((8, REGION), jnp.float32)
        sums = lax.fori_loop(0, BLOCK // 8, chunk, (zero,) * (ORDER * ORDER), unroll=4)
        for n in range(ORDER * ORDER):
            partial[pl.ds(pl.multiple_of((i * ORDER * ORDER + n) * 8, 8), 8), :] = sums[n]
        return carry

    lax.fori_loop(0, ORDER, along, 0)
    count = out_ref.shape[0]
    total = partial[pl.ds(0, count, stride=8), :]
    for s in range(1, 8):
        total += partial[pl.ds(s, count, stride=8), :]
    out_ref[...] = total


def moments_kernel(bodies_ref, out_ref, turned_ref, px, py, pz, partial):
    gather_moments(bodies_ref, out_ref, turned_ref, px, py, pz, partial)


def swapped_moments_kernel(
    counts_ref, bodies_ref, got0_ref, got1_ref, got2_ref, out_ref, turned_ref, merged, px, py, pz, partial
):
    column = lax.broadcasted_iota(jnp.int32, (REGION, BLOCK), 0) * BLOCK + lax.broadcasted_iota(
        jnp.int32, (REGION, BLOCK), 1
    )
    for rnd, got in enumerate((got0_ref, got1_ref, got2_ref)):

        @pl.when(pl.program_id(0) == rnd)
        def _():
            keep = column < counts_ref[rnd]
            for dim in range(4):
                merged[dim] = jnp.where(keep, got[dim], bodies_ref[dim])

    gather_moments(merged, out_ref, turned_ref, px, py, pz, partial)


def moment_scratch(nodes_count):
    return [pltpu.VMEM((ORDER, BLOCK, REGION), jnp.float32) for _ in range(3)] + [
        pltpu.VMEM((8 * nodes_count, REGION), jnp.float32)
    ]


def coefficients_kernel(
    send_ref, swapped_ref, stayed_ref, leaf_ref, compress_ref, own_ref, got_ref, padded, packed, send_sem, recv_sem
):
    leaves = own_ref.shape[0]
    peers = got_ref.shape[0] // 16
    subs = lax.axis_size("sub")
    me = lax.axis_index("space") * subs + lax.axis_index("sub")
    barrier = pltpu.get_barrier_semaphore()

    def greet(hop, carry):
        peer = lax.rem(me + hop, peers)
        pl.semaphore_signal(
            barrier, inc=1, device_id=(peer // subs, lax.rem(peer, subs)), device_id_type=pl.DeviceIdType.MESH
        )
        return carry

    lax.fori_loop(1, peers, greet, 0)
    total = jnp.zeros((leaves, 2 * RANK), jnp.float32)
    at = 0
    for sums in (swapped_ref, stayed_ref):
        count = sums.shape[1]
        ids = leaf_ref[:, pl.ds(at, count)]
        onehot = lax.broadcasted_iota(jnp.int32, (leaves, count), 0) == ids
        onehot = jnp.where(onehot, 1.0, 0.0).astype(jnp.bfloat16)
        moved = jnp.dot(
            compress_ref[...], sums[...], precision=lax.Precision.HIGHEST, preferred_element_type=jnp.float32
        )
        both = jnp.concatenate(split_two(moved), axis=0)
        total += lax.dot_general(onehot, both, (((1,), (1,)), ((), ())), preferred_element_type=jnp.float32)
        at += count
    own = (total + pltpu.roll(total, RANK, 1)).astype(jnp.bfloat16).astype(jnp.float32)
    own_ref[...] = own
    padded[pl.ds(0, 8), :] = jnp.zeros((8, 2 * RANK), jnp.float32)
    padded[pl.ds(8, leaves), :] = own
    padded[pl.ds(8 + leaves, 8), :] = jnp.zeros((8, 2 * RANK), jnp.float32)
    row_of = lax.broadcasted_iota(jnp.int32, (8, 2 * RANK), 0)
    low = lax.broadcasted_iota(jnp.int32, (8, 2 * RANK), 1) < RANK

    def pack(peer):
        line = send_ref.at[pl.ds(peer * 32, 32)]
        halves = []
        for start in (0, 8):
            rows = None
            for j in range(8):
                slot = 2 * (start + j)
                both = jnp.where(low, padded[pl.ds(line[slot], 8), :], padded[pl.ds(line[slot + 1], 8), :])
                rows = both if rows is None else jnp.where(row_of == j, both, rows)
            halves.append(rows)
        return jnp.concatenate(halves, axis=0).astype(jnp.bfloat16)

    def send(hop, carry):
        peer = lax.rem(me + hop, peers)
        at = pl.ds(pl.multiple_of(peer * 16, 16), 16)
        packed[at, :] = pack(peer)
        pltpu.make_async_remote_copy(
            src_ref=packed.at[at, :],
            dst_ref=got_ref.at[mine, :],
            send_sem=send_sem,
            recv_sem=recv_sem,
            device_id=(peer // subs, lax.rem(peer, subs)),
            device_id_type=pl.DeviceIdType.MESH,
        ).start()
        return carry

    mine = pl.ds(pl.multiple_of(me * 16, 16), 16)
    got_ref[mine, :] = pack(me)
    pl.semaphore_wait(barrier, peers - 1)
    lax.fori_loop(1, peers, send, 0)
    others = pl.ds(0, (peers - 1) * 16)
    everything = pltpu.make_async_remote_copy(
        src_ref=packed.at[others, :],
        dst_ref=got_ref.at[others, :],
        send_sem=send_sem,
        recv_sem=recv_sem,
        device_id=(lax.axis_index("space"), lax.axis_index("sub")),
        device_id_type=pl.DeviceIdType.MESH,
    )
    everything.wait_send()
    everything.wait_recv()


def translate_kernel(leaves, inter, src_ref, off_ref, own_ref, ghost_ref, kernels_ref, out_ref, tab, iota, held, placed, m2l_ref, sem):
    step = pl.program_id(0)
    last = pl.num_programs(0) - 1
    rows = (tab.shape[0] - 16) // 2
    ghosts = ghost_ref.shape[0]

    @pl.when(step == 0)
    def _():
        width = kernels_ref.shape[1]
        copy = pltpu.make_async_copy(kernels_ref, m2l_ref.at[:, pl.ds(0, width)], sem)
        copy.start()
        m2l_ref[:, pl.ds(width, m2l_ref.shape[1] - width)] = jnp.zeros(
            (m2l_ref.shape[0], m2l_ref.shape[1] - width), jnp.bfloat16
        )
        iota[...] = lax.broadcasted_iota(jnp.int32, iota.shape, 0).astype(jnp.float32).astype(jnp.bfloat16)
        held[...] = jnp.zeros_like(held)
        tab[pl.ds(0, 8), :] = jnp.zeros((8, 128), jnp.float32)
        tab[pl.ds(2 * rows + 8, 8), :] = jnp.zeros((8, 128), jnp.float32)
        low = lax.broadcasted_iota(jnp.int32, (leaves, 128), 1) < 64
        own = own_ref[...]
        tab[pl.ds(8, leaves), :] = jnp.where(low, own, 0.0)
        tab[pl.ds(8 + rows, leaves), :] = jnp.where(low, 0.0, own)
        low = lax.broadcasted_iota(jnp.int32, (ghosts, 128), 1) < 64
        got = ghost_ref[...].astype(jnp.float32)
        turned = pltpu.roll(got, 64, 1)
        tab[pl.ds(8 + leaves, ghosts), :] = jnp.where(low, got, 0.0)
        tab[pl.ds(8 + leaves + ghosts, ghosts), :] = jnp.where(low, turned, 0.0)
        tab[pl.ds(8 + rows + leaves, ghosts), :] = jnp.where(low, 0.0, turned)
        tab[pl.ds(8 + rows + leaves + ghosts, ghosts), :] = jnp.where(low, 0.0, got)
        copy.wait()

    now = lax.rem(step, 2) * (PAIRS * PITCH)
    before = lax.rem(step + 1, 2) * (PAIRS * PITCH)
    lane_of = lax.broadcasted_iota(jnp.int32, (8, 128), 0)

    def collect(cells, slots):
        lines = [src_ref.at[pl.ds(cell * SLOTS, SLOTS)] for cell in cells]
        for pack in range(SLOTS // 16):
            parts = [[] for _ in cells]
            for start in (pack * 16, pack * 16 + 8):
                totals = [None] * len(cells)
                for j in range(min(8, inter - start)):
                    for u, line in enumerate(lines):
                        window = tab[pl.ds(line[start + j], 8), :]
                        totals[u] = window if j == 0 else jnp.where(lane_of == j, window, totals[u])
                for u in range(len(cells)):
                    parts[u].append(totals[u])
            for u, slot in enumerate(slots):
                held[slot, pl.ds(pack * 16, 16), :] = jnp.concatenate(parts[u], axis=0).astype(jnp.bfloat16)

    def pick(cell, rows_of):
        line = jnp.broadcast_to(off_ref[pl.ds(cell, 1), :], (16, 256)).astype(jnp.bfloat16)
        line = jnp.concatenate([line] * (PAIRS // 16), axis=0)
        chosen = jnp.where(iota[...] == line, jnp.bfloat16(1), jnp.bfloat16(0))
        return jnp.dot(chosen, rows_of, preferred_element_type=jnp.float32)

    def contract(tile, count):
        pieces = []
        for t in range(2 * count):
            at = before + (2 * tile + t) * PITCH
            pieces.append(placed[pl.ds(at, GROUP), :].astype(jnp.bfloat16))
        both = jnp.concatenate(pieces, axis=1)
        kern = m2l_ref[:, pl.ds(pl.multiple_of(tile * 256, 256), 256 * count)]
        return lax.dot_general(both, kern, (((1,), (1,)), ((), ())), preferred_element_type=jnp.float32)

    out_ref[...] = jnp.zeros_like(out_ref)

    @pl.when(step < last)
    def _():
        def body(it, carry):
            cell = UNROLL * it
            part = contract(cell, UNROLL)
            olds = [held[u] for u in range(UNROLL)]
            results = []
            for u in range(UNROLL):
                back = jnp.where(it == 0, GROUP - UNROLL, cell - UNROLL) + u
                results.append((back, pick(back, olds[u])))
            collect([cell + u for u in range(UNROLL)], list(range(UNROLL)))
            for back, result in results:
                placed[pl.ds(now + back, PAIRS, stride=PITCH), :] = result
            out_ref[...] += part
            return carry
        lax.fori_loop(0, GROUP // UNROLL, body, 0)
        for u in range(UNROLL):
            back = GROUP - UNROLL + u
            placed[pl.ds(now + back, PAIRS, stride=PITCH), :] = pick(back, held[u])

    @pl.when(step == last)
    def _():
        def body(it, carry):
            out_ref[...] += contract(it * UNROLL, UNROLL)
            return carry
        lax.fori_loop(0, GROUP // UNROLL, body, 0)


def translate(own, ghost, sources, offsets, m2l_kernels):
    leaves, inter = sources.shape
    ghosts = ghost.shape[0]
    rows = leaves + 2 * ghosts
    remote = sources - leaves
    row = jnp.where(remote < 0, sources, leaves + lax.shift_right_arithmetic(remote, 1) + (remote & 1) * ghosts)
    row = row + (offsets & 1) * rows
    row = row + 8 - jnp.arange(inter, dtype=jnp.int32)[None, :] % 8
    row = jnp.pad(row, ((0, 0), (0, SLOTS - inter))).reshape(-1)
    pair = jnp.pad((offsets >> 1).astype(jnp.float32), ((0, 0), (0, 256 - inter)), constant_values=-1.0)
    steps = leaves // GROUP
    return pl.pallas_call(
        functools.partial(translate_kernel, leaves, inter),
        grid=(steps + 1,),
        in_specs=[
            pl.BlockSpec((GROUP * SLOTS,), lambda i: (jnp.minimum(i, steps - 1),), memory_space=pltpu.SMEM),
            pl.BlockSpec((GROUP, 256), lambda i: (jnp.minimum(i, steps - 1), 0)),
            pl.BlockSpec(own.shape, lambda i: (0, 0)),
            pl.BlockSpec(ghost.shape, lambda i: (0, 0)),
            pl.BlockSpec(memory_space=pl.ANY),
        ],
        out_specs=pl.BlockSpec((GROUP, 64), lambda i: (jnp.maximum(i - 1, 0), 0)),
        out_shape=jax.ShapeDtypeStruct((leaves, 64), jnp.float32),
        scratch_shapes=[
            pltpu.VMEM((2 * rows + 16, 128), jnp.float32),
            pltpu.VMEM((PAIRS, 256), jnp.bfloat16),
            pltpu.VMEM((UNROLL, 256, 128), jnp.bfloat16),
            pltpu.VMEM((2 * PAIRS * PITCH, 128), jnp.float32),
            pltpu.VMEM((RANK, PAIRS * 128), jnp.bfloat16),
            pltpu.SemaphoreType.DMA,
        ],
        compiler_params=params(),
    )(row, pair, own, ghost, m2l_kernels)


def evaluate_kernel(swapped_ref, stayed_ref, leaf_ref, local_ref, expand_ref, out_ref, bodies, nodes, result):
    step = pl.program_id(0)
    leaves = local_ref.shape[0]
    count = expand_ref.shape[0]

    @pl.when(step == 0)
    def _():
        full = lax.dot_general(
            expand_ref[...],
            local_ref[...],
            (((1,), (1,)), ((), ())),
            precision=lax.Precision.HIGHEST,
            preferred_element_type=jnp.float32,
        )
        parts = jnp.concatenate(split_two(full), axis=0)
        for region in range(nodes.shape[0]):
            ids = leaf_ref[:, pl.ds(region * REGION, REGION)]
            onehot = lax.broadcasted_iota(jnp.int32, (leaves, REGION), 0) == ids
            onehot = jnp.where(onehot, 1.0, 0.0).astype(jnp.bfloat16)
            picked = jnp.dot(parts, onehot, preferred_element_type=jnp.float32)
            nodes[region] = picked[:count] + picked[count:]

    @pl.when(step < SWAPS)
    def _():
        bodies[...] = swapped_ref[...]

    @pl.when(step >= SWAPS)
    def _():
        bodies[...] = stayed_ref[...]

    def chunk(v, carry):
        at = pl.ds(pl.multiple_of(v * 16, 16), 16)
        px, py, pz = (chebyshev(bodies[dim, at, :]) for dim in range(3))
        value = None
        for i in range(ORDER):
            middle = None
            for j in range(ORDER):
                first = (i * ORDER + j) * ORDER
                inner = nodes[step, pl.ds(first + 1, 1), :] * pz[0] + nodes[step, pl.ds(first, 1), :]
                for k in range(2, ORDER):
                    inner += nodes[step, pl.ds(first + k, 1), :] * pz[k - 1]
                middle = inner if j == 0 else middle + inner * py[j - 1]
            value = middle if i == 0 else value + middle * px[i - 1]
        result[at, :] = value
        return carry

    lax.fori_loop(0, BLOCK // 16, chunk, 0)
    out_ref[...] = result[...].T


def on_device(
    coords,
    masses,
    swap_counts,
    leaf_of_block,
    let_send,
    inter_source,
    inter_offset,
    compress,
    m2l_kernels,
    expand,
):
    nodes_count = compress.shape[0]
    leaves = inter_source.shape[0]
    local_bodies = coords.shape[1]
    blocks = local_bodies // BLOCK
    regions = blocks // REGION
    peers, per_peer = let_send.shape[1:]
    bodies = jnp.concatenate([coords.reshape(3, blocks, BLOCK), masses.reshape(1, blocks, BLOCK)], axis=0)
    top_bit = lax.axis_size("space").bit_length() - 2
    got_outer = from_partner(bodies[:, 0:REGION], "space", top_bit)
    got_inner = from_partner(bodies[:, REGION : 2 * REGION], "space", 0)
    got_sub = from_partner(bodies[:, 2 * REGION : 3 * REGION], "sub", 0)
    block4 = (4, REGION, BLOCK)
    sums_spec = pl.BlockSpec((nodes_count, REGION), lambda g: (0, g))
    turned_spec = pl.BlockSpec((3, BLOCK, REGION), lambda g: (0, 0, g))
    stays = regions - SWAPS
    stayed, stayed_turned = pl.pallas_call(
        moments_kernel,
        grid=(stays,),
        in_specs=[pl.BlockSpec(block4, lambda g: (0, g + SWAPS, 0))],
        out_specs=[sums_spec, turned_spec],
        out_shape=[
            jax.ShapeDtypeStruct((nodes_count, stays * REGION), jnp.float32),
            jax.ShapeDtypeStruct((3, BLOCK, stays * REGION), jnp.float32),
        ],
        scratch_shapes=moment_scratch(nodes_count),
        compiler_params=params(),
        cost_estimate=pl.CostEstimate(flops=50_000_000, bytes_accessed=4_000_000, transcendentals=0),
    )(bodies)
    whole4 = pl.BlockSpec(block4, lambda g: (0, 0, 0))
    swapped, swapped_turned = pl.pallas_call(
        swapped_moments_kernel,
        grid=(SWAPS,),
        in_specs=[
            pl.BlockSpec(memory_space=pltpu.SMEM),
            pl.BlockSpec(block4, lambda g: (0, g, 0)),
            whole4,
            whole4,
            whole4,
        ],
        out_specs=[sums_spec, turned_spec],
        out_shape=[
            jax.ShapeDtypeStruct((nodes_count, SWAPS * REGION), jnp.float32),
            jax.ShapeDtypeStruct((3, BLOCK, SWAPS * REGION), jnp.float32),
        ],
        scratch_shapes=[pltpu.VMEM(block4, jnp.float32)] + moment_scratch(nodes_count),
        compiler_params=params(),
    )(swap_counts.reshape(SWAPS), bodies, got_outer, got_inner, got_sub)
    basis = node_basis()
    exact = functools.partial(jnp.dot, precision=lax.Precision.HIGHEST, preferred_element_type=jnp.float32)
    compress_polys = exact(compress.T, basis)
    expand_polys = exact(basis.T, expand.T)
    leaf_row = leaf_of_block.reshape(1, blocks)
    send = let_send.reshape(peers, per_peer) + 8 - (jnp.arange(per_peer, dtype=jnp.int32)[None, :] // 2) % 8
    vmem = pl.BlockSpec(memory_space=pltpu.VMEM)
    own, incoming = pl.pallas_call(
        coefficients_kernel,
        in_specs=[pl.BlockSpec(memory_space=pltpu.SMEM), vmem, vmem, vmem, vmem],
        out_specs=[vmem, vmem],
        out_shape=[
            jax.ShapeDtypeStruct((leaves, 2 * RANK), jnp.float32),
            jax.ShapeDtypeStruct((peers * per_peer // 2, 2 * RANK), jnp.bfloat16),
        ],
        scratch_shapes=[
            pltpu.VMEM((leaves + 16, 2 * RANK), jnp.float32),
            pltpu.VMEM((peers * per_peer // 2, 2 * RANK), jnp.bfloat16),
            pltpu.SemaphoreType.DMA,
            pltpu.SemaphoreType.DMA,
        ],
        compiler_params=params(collective_id=0, has_side_effects=True),
    )(send.reshape(-1), swapped, stayed, leaf_row, compress_polys)
    local = translate(own, incoming, inter_source, inter_offset, m2l_kernels)
    values = pl.pallas_call(
        evaluate_kernel,
        grid=(regions,),
        in_specs=[
            pl.BlockSpec((3, BLOCK, REGION), lambda g: (0, 0, jnp.minimum(g, SWAPS - 1))),
            pl.BlockSpec((3, BLOCK, REGION), lambda g: (0, 0, jnp.maximum(g - SWAPS, 0))),
            pl.BlockSpec((1, blocks), lambda g: (0, 0)),
            pl.BlockSpec((leaves, RANK), lambda g: (0, 0)),
            pl.BlockSpec((nodes_count, RANK), lambda g: (0, 0)),
        ],
        out_specs=pl.BlockSpec((REGION, BLOCK), lambda g: (g, 0)),
        out_shape=jax.ShapeDtypeStruct((blocks, BLOCK), jnp.float32),
        scratch_shapes=[
            pltpu.VMEM((3, BLOCK, REGION), jnp.float32),
            pltpu.VMEM((regions, nodes_count, REGION), jnp.float32),
            pltpu.VMEM((BLOCK, REGION), jnp.float32),
        ],
        compiler_params=params(),
    )(swapped_turned, stayed_turned, leaf_row, local, expand_polys)
    return values.reshape(local_bodies)


def solution(mesh):
    return jax.shard_map(
        on_device,
        mesh=mesh,
        in_specs=(
            P(None, ("space", "sub")),
            P(("space", "sub")),
            P(("space", "sub"), None),
            P(("space", "sub")),
            P(("space", "sub"), None, None),
            P(("space", "sub"), None),
            P(("space", "sub"), None),
            P(),
            P(),
            P(),
        ),
        out_specs=P(("space", "sub")),
        check_vma=False,
    )
```

```python
import functools

import jax
import jax.numpy as jnp
import numpy as np
from jax import lax
from jax.experimental import pallas as pl
from jax.experimental.pallas import tpu as pltpu
from jax.sharding import PartitionSpec as P

ORDER = 6
RANK = 64
BLOCK = 128
REGION = 128
SWAPS = 3
GROUP = 80
SLOTS = 192
PAIRS = 160
PITCH = 81
UNROLL = 8
STRIDE = 9


def params(**more):
    return pltpu.CompilerParams(vmem_limit_bytes=56 << 20, **more)


def from_partner(block, axis, distance):
    count = lax.axis_size(axis)
    route = []
    for low in range(count):
        high = low | 1 << distance
        if high != low and high < count:
            route += [(low, high), (high, low)]
    return lax.ppermute(block, axis, route)


def chebyshev(points):
    twice = 2.0 * points
    polys = [points, twice * points - 1.0]
    for _ in range(ORDER - 3):
        polys.append(twice * polys[-1] - polys[-2])
    return polys


def node_basis():
    single = np.zeros((ORDER, ORDER))
    for j in range(ORDER):
        for k in range(ORDER):
            single[j, k] = np.cos(k * (2 * j + 1) * np.pi / (2 * ORDER)) * (1.0 if k == 0 else 2.0) / ORDER
    return np.kron(np.kron(single, single), single).astype(np.float32)


def split_two(values):
    first = values.astype(jnp.bfloat16)
    return first, (values - first.astype(jnp.float32)).astype(jnp.bfloat16)


def gather_moments(coords, masses, out_ref, turned_ref, px, py, pz, partial):
    mass = masses[...].T
    px[0] = mass
    for dim, scratch in enumerate((px, py, pz)):
        points = coords[dim].T
        turned_ref[dim] = points
        for k, poly in enumerate(chebyshev(points)):
            scratch[k + 1] = poly * mass if dim == 0 else poly

    def along(i, carry):
        def chunk(v, sums):
            at = pl.ds(pl.multiple_of(v * 8, 8), 8)
            left = px[i, at, :]
            inner = [pz[k, at, :] for k in range(1, ORDER)]
            new = []
            for j in range(ORDER):
                pair = left if j == 0 else left * py[j, at, :]
                new.append(sums[j * ORDER] + pair)
                for k in range(1, ORDER):
                    new.append(sums[j * ORDER + k] + pair * inner[k - 1])
            return tuple(new)

        zero = jnp.zeros((8, REGION), jnp.float32)
        sums = lax.fori_loop(0, BLOCK // 8, chunk, (zero,) * (ORDER * ORDER), unroll=4)
        for n in range(ORDER * ORDER):
            partial[pl.ds((i * ORDER * ORDER + n) * STRIDE, 8), :] = sums[n]
        return carry

    lax.fori_loop(0, ORDER, along, 0)
    count = out_ref.shape[0]
    total = partial[pl.ds(0, count, stride=STRIDE), :]
    for s in range(1, 8):
        total += partial[pl.ds(s, count, stride=STRIDE), :]
    out_ref[...] = total


def moments_kernel(coords_ref, masses_ref, out_ref, turned_ref, px, py, pz, partial):
    gather_moments(coords_ref, masses_ref, out_ref, turned_ref, px, py, pz, partial)


def swapped_moments_kernel(
    counts_ref,
    coords_ref,
    masses_ref,
    got0_ref,
    got1_ref,
    got2_ref,
    out_ref,
    turned_ref,
    coords,
    masses,
    px,
    py,
    pz,
    partial,
):
    column = lax.broadcasted_iota(jnp.int32, (REGION, BLOCK), 0) * BLOCK + lax.broadcasted_iota(
        jnp.int32, (REGION, BLOCK), 1
    )
    for rnd, got in enumerate((got0_ref, got1_ref, got2_ref)):

        @pl.when(pl.program_id(0) == rnd)
        def _():
            keep = column < counts_ref[rnd]
            for dim in range(3):
                coords[dim] = jnp.where(keep, got[dim], coords_ref[dim])
            masses[...] = jnp.where(keep, got[3], masses_ref[...])

    gather_moments(coords, masses, out_ref, turned_ref, px, py, pz, partial)


def moment_scratch(nodes_count):
    return [pltpu.VMEM((ORDER, BLOCK, REGION), jnp.float32) for _ in range(3)] + [
        pltpu.VMEM((STRIDE * nodes_count, REGION), jnp.float32)
    ]


def coefficients_kernel(
    send_ref, swapped_ref, stayed_ref, leaf_ref, compress_ref, own_ref, got_ref, padded, packed, send_sem, recv_sem
):
    leaves = own_ref.shape[0]
    peers = got_ref.shape[0] // 16
    subs = lax.axis_size("sub")
    me = lax.axis_index("space") * subs + lax.axis_index("sub")
    barrier = pltpu.get_barrier_semaphore()

    def greet(hop, carry):
        peer = lax.rem(me + hop, peers)
        pl.semaphore_signal(
            barrier, inc=1, device_id=(peer // subs, lax.rem(peer, subs)), device_id_type=pl.DeviceIdType.MESH
        )
        return carry

    lax.fori_loop(1, peers, greet, 0)
    total = jnp.zeros((leaves, 2 * RANK), jnp.float32)
    at = 0
    for sums in (swapped_ref, stayed_ref):
        count = sums.shape[1]
        ids = leaf_ref[:, pl.ds(at, count)]
        onehot = lax.broadcasted_iota(jnp.int32, (leaves, count), 0) == ids
        onehot = jnp.where(onehot, 1.0, 0.0).astype(jnp.bfloat16)
        moved = jnp.dot(
            compress_ref[...], sums[...], precision=lax.Precision.HIGHEST, preferred_element_type=jnp.float32
        )
        both = jnp.concatenate(split_two(moved), axis=0)
        total += lax.dot_general(onehot, both, (((1,), (1,)), ((), ())), preferred_element_type=jnp.float32)
        at += count
    own = (total + pltpu.roll(total, RANK, 1)).astype(jnp.bfloat16).astype(jnp.float32)
    own_ref[...] = own
    padded[pl.ds(0, 8), :] = jnp.zeros((8, 2 * RANK), jnp.float32)
    padded[pl.ds(8, leaves), :] = own
    padded[pl.ds(8 + leaves, 8), :] = jnp.zeros((8, 2 * RANK), jnp.float32)
    row_of = lax.broadcasted_iota(jnp.int32, (8, 2 * RANK), 0)
    low = lax.broadcasted_iota(jnp.int32, (8, 2 * RANK), 1) < RANK

    def pack(peer):
        line = send_ref.at[pl.ds(peer * 32, 32)]
        halves = []
        for start in (0, 8):
            rows = None
            for j in range(8):
                slot = 2 * (start + j)
                both = jnp.where(low, padded[pl.ds(line[slot], 8), :], padded[pl.ds(line[slot + 1], 8), :])
                rows = both if rows is None else jnp.where(row_of == j, both, rows)
            halves.append(rows)
        return jnp.concatenate(halves, axis=0).astype(jnp.bfloat16)

    def send(hop, carry):
        peer = lax.rem(me + hop, peers)
        at = pl.ds(pl.multiple_of(peer * 16, 16), 16)
        packed[at, :] = pack(peer)
        pltpu.make_async_remote_copy(
            src_ref=packed.at[at, :],
            dst_ref=got_ref.at[mine, :],
            send_sem=send_sem,
            recv_sem=recv_sem,
            device_id=(peer // subs, lax.rem(peer, subs)),
            device_id_type=pl.DeviceIdType.MESH,
        ).start()
        return carry

    mine = pl.ds(pl.multiple_of(me * 16, 16), 16)
    got_ref[mine, :] = pack(me)
    pl.semaphore_wait(barrier, peers - 1)
    lax.fori_loop(1, peers, send, 0)
    others = pl.ds(0, (peers - 1) * 16)
    everything = pltpu.make_async_remote_copy(
        src_ref=packed.at[others, :],
        dst_ref=got_ref.at[others, :],
        send_sem=send_sem,
        recv_sem=recv_sem,
        device_id=(lax.axis_index("space"), lax.axis_index("sub")),
        device_id_type=pl.DeviceIdType.MESH,
    )
    everything.wait_send()
    everything.wait_recv()


def translate_kernel(leaves, inter, src_ref, off_ref, own_ref, ghost_ref, kernels_ref, out_ref, tab, iota, held, placed, m2l_ref, sem):
    step = pl.program_id(0)
    last = pl.num_programs(0) - 1
    rows = (tab.shape[0] - 16) // 2
    ghosts = ghost_ref.shape[0]

    @pl.when(step == 0)
    def _():
        width = kernels_ref.shape[1]
        copy = pltpu.make_async_copy(kernels_ref, m2l_ref.at[:, pl.ds(0, width)], sem)
        copy.start()
        m2l_ref[:, pl.ds(width, m2l_ref.shape[1] - width)] = jnp.zeros(
            (m2l_ref.shape[0], m2l_ref.shape[1] - width), jnp.bfloat16
        )
        iota[...] = lax.broadcasted_iota(jnp.int32, iota.shape, 0).astype(jnp.float32).astype(jnp.bfloat16)
        held[...] = jnp.zeros_like(held)
        tab[pl.ds(0, 8), :] = jnp.zeros((8, 128), jnp.float32)
        tab[pl.ds(2 * rows + 8, 8), :] = jnp.zeros((8, 128), jnp.float32)
        low = lax.broadcasted_iota(jnp.int32, (leaves, 128), 1) < 64
        own = own_ref[...]
        tab[pl.ds(8, leaves), :] = jnp.where(low, own, 0.0)
        tab[pl.ds(8 + rows, leaves), :] = jnp.where(low, 0.0, own)
        low = lax.broadcasted_iota(jnp.int32, (ghosts, 128), 1) < 64
        got = ghost_ref[...].astype(jnp.float32)
        turned = pltpu.roll(got, 64, 1)
        tab[pl.ds(8 + leaves, ghosts), :] = jnp.where(low, got, 0.0)
        tab[pl.ds(8 + leaves + ghosts, ghosts), :] = jnp.where(low, turned, 0.0)
        tab[pl.ds(8 + rows + leaves, ghosts), :] = jnp.where(low, 0.0, turned)
        tab[pl.ds(8 + rows + leaves + ghosts, ghosts), :] = jnp.where(low, 0.0, got)
        copy.wait()

    now = lax.rem(step, 2) * (PAIRS * PITCH)
    before = lax.rem(step + 1, 2) * (PAIRS * PITCH)
    lane_of = lax.broadcasted_iota(jnp.int32, (8, 128), 0)

    def collect(cells, slots):
        lines = [src_ref.at[pl.ds(cell * SLOTS, SLOTS)] for cell in cells]
        for pack in range(SLOTS // 16):
            parts = [[] for _ in cells]
            for start in (pack * 16, pack * 16 + 8):
                totals = [None] * len(cells)
                for j in range(min(8, inter - start)):
                    for u, line in enumerate(lines):
                        window = tab[pl.ds(line[start + j], 8), :]
                        totals[u] = window if j == 0 else jnp.where(lane_of == j, window, totals[u])
                for u in range(len(cells)):
                    parts[u].append(totals[u])
            for u, slot in enumerate(slots):
                held[slot, pl.ds(pack * 16, 16), :] = jnp.concatenate(parts[u], axis=0).astype(jnp.bfloat16)

    def pick(cell, rows_of):
        line = jnp.broadcast_to(off_ref[pl.ds(cell, 1), :], (16, 256)).astype(jnp.bfloat16)
        line = jnp.concatenate([line] * (PAIRS // 16), axis=0)
        chosen = jnp.where(iota[...] == line, jnp.bfloat16(1), jnp.bfloat16(0))
        return jnp.dot(chosen[:, :SLOTS], rows_of, preferred_element_type=jnp.float32)

    def contract(tile, count):
        pieces = []
        for t in range(2 * count):
            at = before + (2 * tile + t) * PITCH
            pieces.append(placed[pl.ds(at, GROUP), :].astype(jnp.bfloat16))
        both = jnp.concatenate(pieces, axis=1)
        kern = m2l_ref[:, pl.ds(pl.multiple_of(tile * 256, 256), 256 * count)]
        return lax.dot_general(both, kern, (((1,), (1,)), ((), ())), preferred_element_type=jnp.float32)

    out_ref[...] = jnp.zeros_like(out_ref)

    @pl.when(step < last)
    def _():
        def body(it, carry):
            cell = UNROLL * it
            part = contract(cell, UNROLL)
            olds = [held[u] for u in range(UNROLL)]
            results = []
            for u in range(UNROLL):
                back = jnp.where(it == 0, GROUP - UNROLL, cell - UNROLL) + u
                results.append((back, pick(back, olds[u])))
            collect([cell + u for u in range(UNROLL)], list(range(UNROLL)))
            for back, result in results:
                placed[pl.ds(now + back, PAIRS, stride=PITCH), :] = result
            out_ref[...] += part
            return carry
        lax.fori_loop(0, GROUP // UNROLL, body, 0)
        for u in range(UNROLL):
            back = GROUP - UNROLL + u
            placed[pl.ds(now + back, PAIRS, stride=PITCH), :] = pick(back, held[u])

    @pl.when(step == last)
    def _():
        def body(it, carry):
            out_ref[...] += contract(it * UNROLL, UNROLL)
            return carry
        lax.fori_loop(0, GROUP // UNROLL, body, 0)


def translate(own, ghost, sources, offsets, m2l_kernels):
    leaves, inter = sources.shape
    ghosts = ghost.shape[0]
    rows = leaves + 2 * ghosts
    remote = sources - leaves
    row = jnp.where(remote < 0, sources, leaves + lax.shift_right_arithmetic(remote, 1) + (remote & 1) * ghosts)
    row = row + (offsets & 1) * rows
    row = row + 8 - jnp.arange(inter, dtype=jnp.int32)[None, :] % 8
    row = jnp.pad(row, ((0, 0), (0, SLOTS - inter))).reshape(-1)
    pair = jnp.pad((offsets >> 1).astype(jnp.float32), ((0, 0), (0, 256 - inter)), constant_values=-1.0)
    steps = leaves // GROUP
    return pl.pallas_call(
        functools.partial(translate_kernel, leaves, inter),
        grid=(steps + 1,),
        in_specs=[
            pl.BlockSpec((GROUP * SLOTS,), lambda i: (jnp.minimum(i, steps - 1),), memory_space=pltpu.SMEM),
            pl.BlockSpec((GROUP, 256), lambda i: (jnp.minimum(i, steps - 1), 0)),
            pl.BlockSpec(own.shape, lambda i: (0, 0)),
            pl.BlockSpec(ghost.shape, lambda i: (0, 0)),
            pl.BlockSpec(memory_space=pl.ANY),
        ],
        out_specs=pl.BlockSpec((GROUP, 64), lambda i: (jnp.maximum(i - 1, 0), 0)),
        out_shape=jax.ShapeDtypeStruct((leaves, 64), jnp.float32),
        scratch_shapes=[
            pltpu.VMEM((2 * rows + 16, 128), jnp.float32),
            pltpu.VMEM((PAIRS, 256), jnp.bfloat16),
            pltpu.VMEM((UNROLL, SLOTS, 128), jnp.bfloat16),
            pltpu.VMEM((2 * PAIRS * PITCH, 128), jnp.float32),
            pltpu.VMEM((RANK, PAIRS * 128), jnp.bfloat16),
            pltpu.SemaphoreType.DMA,
        ],
        compiler_params=params(),
    )(row, pair, own, ghost, m2l_kernels)


def evaluate_kernel(swapped_ref, stayed_ref, leaf_ref, local_ref, expand_ref, out_ref, bodies, nodes, result):
    step = pl.program_id(0)
    leaves = local_ref.shape[0]

    @pl.when(step == 0)
    def _():
        local = jnp.concatenate([part.astype(jnp.float32) for part in split_two(local_ref[...])], axis=1)
        local = local.T.astype(jnp.bfloat16)
        large, small = split_two(expand_ref[...])
        expands = jnp.concatenate([large, large, small], axis=1)
        width = 2 * REGION
        for pair in range(nodes.shape[0] // 2):
            ids = leaf_ref[:, pl.ds(pair * width, width)]
            onehot = lax.broadcasted_iota(jnp.int32, (leaves, width), 0) == ids
            onehot = jnp.where(onehot, 1.0, 0.0).astype(jnp.bfloat16)
            picked = jnp.dot(local, onehot, preferred_element_type=jnp.float32).astype(jnp.bfloat16)
            terms = jnp.concatenate([picked, picked[:RANK]], axis=0)
            values = jnp.dot(expands, terms, preferred_element_type=jnp.float32)
            nodes[2 * pair] = values[:, :REGION]
            nodes[2 * pair + 1] = values[:, REGION:]

    @pl.when(step < SWAPS)
    def _():
        bodies[...] = swapped_ref[...]

    @pl.when(step >= SWAPS)
    def _():
        bodies[...] = stayed_ref[...]

    def chunk(v, carry):
        at = pl.ds(pl.multiple_of(v * 16, 16), 16)
        px, py, pz = (chebyshev(bodies[dim, at, :]) for dim in range(3))
        value = None
        for i in range(ORDER):
            middle = None
            for j in range(ORDER):
                first = (i * ORDER + j) * ORDER
                inner = nodes[step, pl.ds(first + 1, 1), :] * pz[0] + nodes[step, pl.ds(first, 1), :]
                for k in range(2, ORDER):
                    inner += nodes[step, pl.ds(first + k, 1), :] * pz[k - 1]
                middle = inner if j == 0 else middle + inner * py[j - 1]
            value = middle if i == 0 else value + middle * px[i - 1]
        result[at, :] = value
        return carry

    lax.fori_loop(0, BLOCK // 16, chunk, 0)
    out_ref[...] = result[...].T


def on_device(
    coords,
    masses,
    swap_counts,
    leaf_of_block,
    let_send,
    inter_source,
    inter_offset,
    compress,
    m2l_kernels,
    expand,
):
    nodes_count = compress.shape[0]
    leaves = inter_source.shape[0]
    local_bodies = coords.shape[1]
    blocks = local_bodies // BLOCK
    regions = blocks // REGION
    peers, per_peer = let_send.shape[1:]
    coords = coords.reshape(3, blocks, BLOCK)
    masses = masses.reshape(blocks, BLOCK)
    top_bit = lax.axis_size("space").bit_length() - 2
    got = []
    for rnd, (axis, distance) in enumerate((("space", top_bit), ("space", 0), ("sub", 0))):
        at = slice(rnd * REGION, (rnd + 1) * REGION)
        got.append(from_partner(jnp.concatenate([coords[:, at], masses[None, at]], axis=0), axis, distance))
    coords_block = (3, REGION, BLOCK)
    masses_block = (REGION, BLOCK)
    sums_spec = pl.BlockSpec((nodes_count, REGION), lambda g: (0, g))
    turned_spec = pl.BlockSpec((3, BLOCK, REGION), lambda g: (0, 0, g))
    stays = regions - SWAPS
    stayed, stayed_turned = pl.pallas_call(
        moments_kernel,
        grid=(stays,),
        in_specs=[
            pl.BlockSpec(coords_block, lambda g: (0, g + SWAPS, 0)),
            pl.BlockSpec(masses_block, lambda g: (g + SWAPS, 0)),
        ],
        out_specs=[sums_spec, turned_spec],
        out_shape=[
            jax.ShapeDtypeStruct((nodes_count, stays * REGION), jnp.float32),
            jax.ShapeDtypeStruct((3, BLOCK, stays * REGION), jnp.float32),
        ],
        scratch_shapes=moment_scratch(nodes_count),
        compiler_params=params(),
        cost_estimate=pl.CostEstimate(flops=50_000_000, bytes_accessed=4_000_000, transcendentals=0),
    )(coords, masses)
    whole4 = pl.BlockSpec((4, REGION, BLOCK), lambda g: (0, 0, 0))
    swapped, swapped_turned = pl.pallas_call(
        swapped_moments_kernel,
        grid=(SWAPS,),
        in_specs=[
            pl.BlockSpec(memory_space=pltpu.SMEM),
            pl.BlockSpec(coords_block, lambda g: (0, g, 0)),
            pl.BlockSpec(masses_block, lambda g: (g, 0)),
            whole4,
            whole4,
            whole4,
        ],
        out_specs=[sums_spec, turned_spec],
        out_shape=[
            jax.ShapeDtypeStruct((nodes_count, SWAPS * REGION), jnp.float32),
            jax.ShapeDtypeStruct((3, BLOCK, SWAPS * REGION), jnp.float32),
        ],
        scratch_shapes=[pltpu.VMEM(coords_block, jnp.float32), pltpu.VMEM(masses_block, jnp.float32)]
        + moment_scratch(nodes_count),
        compiler_params=params(),
    )(swap_counts.reshape(SWAPS), coords, masses, *got)
    basis = node_basis()
    exact = functools.partial(jnp.dot, precision=lax.Precision.HIGHEST, preferred_element_type=jnp.float32)
    compress_polys = exact(compress.T, basis)
    expand_polys = exact(basis.T, expand.T)
    leaf_row = leaf_of_block.reshape(1, blocks)
    send = let_send.reshape(peers, per_peer) + 8 - (jnp.arange(per_peer, dtype=jnp.int32)[None, :] // 2) % 8
    vmem = pl.BlockSpec(memory_space=pltpu.VMEM)
    own, incoming = pl.pallas_call(
        coefficients_kernel,
        in_specs=[pl.BlockSpec(memory_space=pltpu.SMEM), vmem, vmem, vmem, vmem],
        out_specs=[vmem, vmem],
        out_shape=[
            jax.ShapeDtypeStruct((leaves, 2 * RANK), jnp.float32),
            jax.ShapeDtypeStruct((peers * per_peer // 2, 2 * RANK), jnp.bfloat16),
        ],
        scratch_shapes=[
            pltpu.VMEM((leaves + 16, 2 * RANK), jnp.float32),
            pltpu.VMEM((peers * per_peer // 2, 2 * RANK), jnp.bfloat16),
            pltpu.SemaphoreType.DMA,
            pltpu.SemaphoreType.DMA,
        ],
        compiler_params=params(collective_id=0, has_side_effects=True),
    )(send.reshape(-1), swapped, stayed, leaf_row, compress_polys)
    local = translate(own, incoming, inter_source, inter_offset, m2l_kernels)
    values = pl.pallas_call(
        evaluate_kernel,
        grid=(regions,),
        in_specs=[
            pl.BlockSpec((3, BLOCK, REGION), lambda g: (0, 0, jnp.minimum(g, SWAPS - 1))),
            pl.BlockSpec((3, BLOCK, REGION), lambda g: (0, 0, jnp.maximum(g - SWAPS, 0))),
            pl.BlockSpec((1, blocks), lambda g: (0, 0)),
            pl.BlockSpec((leaves, RANK), lambda g: (0, 0)),
            pl.BlockSpec((nodes_count, RANK), lambda g: (0, 0)),
        ],
        out_specs=pl.BlockSpec((REGION, BLOCK), lambda g: (g, 0)),
        out_shape=jax.ShapeDtypeStruct((blocks, BLOCK), jnp.float32),
        scratch_shapes=[
            pltpu.VMEM((3, BLOCK, REGION), jnp.float32),
            pltpu.VMEM((regions, nodes_count, REGION), jnp.float32),
            pltpu.VMEM((BLOCK, REGION), jnp.float32),
        ],
        compiler_params=params(),
    )(swapped_turned, stayed_turned, leaf_row, local, expand_polys)
    return values.reshape(local_bodies)


def solution(mesh):
    return jax.shard_map(
        on_device,
        mesh=mesh,
        in_specs=(
            P(None, ("space", "sub")),
            P(("space", "sub")),
            P(("space", "sub"), None),
            P(("space", "sub")),
            P(("space", "sub"), None, None),
            P(("space", "sub"), None),
            P(("space", "sub"), None),
            P(),
            P(),
            P(),
        ),
        out_specs=P(("space", "sub")),
        check_vma=False,
    )
```

```python
import functools

import jax
import jax.numpy as jnp
import numpy as np
from jax import lax
from jax.experimental import pallas as pl
from jax.experimental.pallas import tpu as pltpu
from jax.sharding import PartitionSpec as P

ORDER = 6
RANK = 64
BLOCK = 128
REGION = 128
SWAPS = 3
GROUP = 80
SLOTS = 192
PAIRS = 160
PITCH = 81
UNROLL = 8
STRIDE = 9


def params(**more):
    return pltpu.CompilerParams(vmem_limit_bytes=56 << 20, **more)


def chebyshev(points):
    twice = 2.0 * points
    polys = [points, twice * points - 1.0]
    for _ in range(ORDER - 3):
        polys.append(twice * polys[-1] - polys[-2])
    return polys


def node_basis():
    single = np.zeros((ORDER, ORDER))
    for j in range(ORDER):
        for k in range(ORDER):
            single[j, k] = np.cos(k * (2 * j + 1) * np.pi / (2 * ORDER)) * (1.0 if k == 0 else 2.0) / ORDER
    return np.kron(np.kron(single, single), single).astype(np.float32)


def split_two(values):
    first = values.astype(jnp.bfloat16)
    return first, (values - first.astype(jnp.float32)).astype(jnp.bfloat16)


def gather_moments(coords, masses, out_ref, turned_ref, px, py, pz, partial):
    mass = masses[...].T
    px[0] = mass
    for dim, scratch in enumerate((px, py, pz)):
        points = coords[dim].T
        turned_ref[dim] = points
        for k, poly in enumerate(chebyshev(points)):
            scratch[k + 1] = poly * mass if dim == 0 else poly

    def along(i, carry):
        def chunk(v, sums):
            at = pl.ds(pl.multiple_of(v * 8, 8), 8)
            left = px[i, at, :]
            inner = [pz[k, at, :] for k in range(1, ORDER)]
            new = []
            for j in range(ORDER):
                pair = left if j == 0 else left * py[j, at, :]
                new.append(sums[j * ORDER] + pair)
                for k in range(1, ORDER):
                    new.append(sums[j * ORDER + k] + pair * inner[k - 1])
            return tuple(new)

        zero = jnp.zeros((8, REGION), jnp.float32)
        sums = lax.fori_loop(0, BLOCK // 8, chunk, (zero,) * (ORDER * ORDER), unroll=4)
        for n in range(ORDER * ORDER):
            partial[pl.ds((i * ORDER * ORDER + n) * STRIDE, 8), :] = sums[n]
        return carry

    lax.fori_loop(0, ORDER, along, 0)
    count = out_ref.shape[0]
    total = partial[pl.ds(0, count, stride=STRIDE), :]
    for s in range(1, 8):
        total += partial[pl.ds(s, count, stride=STRIDE), :]
    out_ref[...] = total


def moments_kernel(
    counts_ref,
    coords_ref,
    masses_ref,
    all_coords,
    all_masses,
    out_ref,
    turned_ref,
    coords,
    masses,
    got,
    send_sem,
    recv_sem,
    px,
    py,
    pz,
    partial,
):
    step = pl.program_id(0)
    stays = pl.num_programs(0) - SWAPS
    space, sub = lax.axis_index("space"), lax.axis_index("sub")
    spaces = lax.axis_size("space")
    partners = (
        (lax.rem(space + spaces // 2, spaces), sub),
        (space + 1 - 2 * lax.rem(space, 2), sub),
        (space, sub + 1 - 2 * lax.rem(sub, 2)),
    )
    column = lax.broadcasted_iota(jnp.int32, (REGION, BLOCK), 0) * BLOCK + lax.broadcasted_iota(
        jnp.int32, (REGION, BLOCK), 1
    )

    def copies(rnd):
        at = pl.ds(rnd * REGION, REGION)
        pairs = ((all_coords.at[:, at, :], got.at[rnd, pl.ds(0, 3)]), (all_masses.at[at, :], got.at[rnd, 3]))
        return [
            pltpu.make_async_remote_copy(
                src_ref=source,
                dst_ref=target,
                send_sem=send_sem.at[2 * rnd + k],
                recv_sem=recv_sem.at[2 * rnd + k],
                device_id=partners[rnd],
                device_id_type=pl.DeviceIdType.MESH,
            )
            for k, (source, target) in enumerate(pairs)
        ]

    @pl.when(step == 0)
    def _():
        barrier = pltpu.get_barrier_semaphore()
        for partner in partners:
            pl.semaphore_signal(barrier, inc=1, device_id=partner, device_id_type=pl.DeviceIdType.MESH)
        pl.semaphore_wait(barrier, SWAPS)
        for rnd in range(SWAPS):
            for copy in copies(rnd):
                copy.start()

    @pl.when(step < stays)
    def _():
        coords[...] = coords_ref[...]
        masses[...] = masses_ref[...]

    for rnd in range(SWAPS):

        @pl.when(step == stays + rnd)
        def _():
            for copy in copies(rnd):
                copy.wait_recv()
            keep = column < counts_ref[rnd]
            for dim in range(3):
                coords[dim] = jnp.where(keep, got[rnd, dim], coords_ref[dim])
            masses[...] = jnp.where(keep, got[rnd, 3], masses_ref[...])

    gather_moments(coords, masses, out_ref, turned_ref, px, py, pz, partial)

    @pl.when(step == stays + SWAPS - 1)
    def _():
        for rnd in range(SWAPS):
            for copy in copies(rnd):
                copy.wait_send()


def moment_scratch(nodes_count):
    return [pltpu.VMEM((ORDER, BLOCK, REGION), jnp.float32) for _ in range(3)] + [
        pltpu.VMEM((STRIDE * nodes_count, REGION), jnp.float32)
    ]


def coefficients_kernel(
    send_ref, sums_ref, leaf_ref, compress_ref, own_ref, got_ref, padded, packed, send_sem, recv_sem
):
    leaves = own_ref.shape[0]
    peers = got_ref.shape[0] // 16
    subs = lax.axis_size("sub")
    me = lax.axis_index("space") * subs + lax.axis_index("sub")
    barrier = pltpu.get_barrier_semaphore()

    def greet(hop, carry):
        peer = lax.rem(me + hop, peers)
        pl.semaphore_signal(
            barrier, inc=1, device_id=(peer // subs, lax.rem(peer, subs)), device_id_type=pl.DeviceIdType.MESH
        )
        return carry

    lax.fori_loop(1, peers, greet, 0)
    onehot = lax.broadcasted_iota(jnp.int32, (leaves, leaf_ref.shape[1]), 0) == leaf_ref[...]
    onehot = jnp.where(onehot, 1.0, 0.0).astype(jnp.bfloat16)
    moved = jnp.dot(
        compress_ref[...], sums_ref[...], precision=lax.Precision.HIGHEST, preferred_element_type=jnp.float32
    )
    both = jnp.concatenate(split_two(moved), axis=0)
    total = lax.dot_general(onehot, both, (((1,), (1,)), ((), ())), preferred_element_type=jnp.float32)
    own = (total + pltpu.roll(total, RANK, 1)).astype(jnp.bfloat16).astype(jnp.float32)
    own_ref[...] = own
    padded[pl.ds(0, 8), :] = jnp.zeros((8, 2 * RANK), jnp.float32)
    padded[pl.ds(8, leaves), :] = own
    padded[pl.ds(8 + leaves, 8), :] = jnp.zeros((8, 2 * RANK), jnp.float32)
    row_of = lax.broadcasted_iota(jnp.int32, (8, 2 * RANK), 0)
    low = lax.broadcasted_iota(jnp.int32, (8, 2 * RANK), 1) < RANK

    def pack(peer):
        line = send_ref.at[pl.ds(peer * 32, 32)]
        halves = []
        for start in (0, 8):
            rows = None
            for j in range(8):
                slot = 2 * (start + j)
                both = jnp.where(low, padded[pl.ds(line[slot], 8), :], padded[pl.ds(line[slot + 1], 8), :])
                rows = both if rows is None else jnp.where(row_of == j, both, rows)
            halves.append(rows)
        return jnp.concatenate(halves, axis=0).astype(jnp.bfloat16)

    def send(hop, carry):
        peer = lax.rem(me + hop, peers)
        at = pl.ds(pl.multiple_of(peer * 16, 16), 16)
        packed[at, :] = pack(peer)
        pltpu.make_async_remote_copy(
            src_ref=packed.at[at, :],
            dst_ref=got_ref.at[mine, :],
            send_sem=send_sem,
            recv_sem=recv_sem,
            device_id=(peer // subs, lax.rem(peer, subs)),
            device_id_type=pl.DeviceIdType.MESH,
        ).start()
        return carry

    mine = pl.ds(pl.multiple_of(me * 16, 16), 16)
    got_ref[mine, :] = pack(me)
    pl.semaphore_wait(barrier, peers - 1)
    lax.fori_loop(1, peers, send, 0)
    others = pl.ds(0, (peers - 1) * 16)
    everything = pltpu.make_async_remote_copy(
        src_ref=packed.at[others, :],
        dst_ref=got_ref.at[others, :],
        send_sem=send_sem,
        recv_sem=recv_sem,
        device_id=(lax.axis_index("space"), lax.axis_index("sub")),
        device_id_type=pl.DeviceIdType.MESH,
    )
    everything.wait_send()
    everything.wait_recv()


def translate_kernel(leaves, inter, src_ref, off_ref, own_ref, ghost_ref, kernels_ref, out_ref, tab, iota, held, placed, m2l_ref, sem):
    step = pl.program_id(0)
    last = pl.num_programs(0) - 1
    rows = (tab.shape[0] - 16) // 2
    ghosts = ghost_ref.shape[0]

    @pl.when(step == 0)
    def _():
        width = kernels_ref.shape[1]
        copy = pltpu.make_async_copy(kernels_ref, m2l_ref.at[:, pl.ds(0, width)], sem)
        copy.start()
        m2l_ref[:, pl.ds(width, m2l_ref.shape[1] - width)] = jnp.zeros(
            (m2l_ref.shape[0], m2l_ref.shape[1] - width), jnp.bfloat16
        )
        iota[...] = lax.broadcasted_iota(jnp.int32, iota.shape, 0).astype(jnp.float32).astype(jnp.bfloat16)
        held[...] = jnp.zeros_like(held)
        tab[pl.ds(0, 8), :] = jnp.zeros((8, 128), jnp.float32)
        tab[pl.ds(2 * rows + 8, 8), :] = jnp.zeros((8, 128), jnp.float32)
        low = lax.broadcasted_iota(jnp.int32, (leaves, 128), 1) < 64
        own = own_ref[...]
        tab[pl.ds(8, leaves), :] = jnp.where(low, own, 0.0)
        tab[pl.ds(8 + rows, leaves), :] = jnp.where(low, 0.0, own)
        low = lax.broadcasted_iota(jnp.int32, (ghosts, 128), 1) < 64
        got = ghost_ref[...].astype(jnp.float32)
        turned = pltpu.roll(got, 64, 1)
        tab[pl.ds(8 + leaves, ghosts), :] = jnp.where(low, got, 0.0)
        tab[pl.ds(8 + leaves + ghosts, ghosts), :] = jnp.where(low, turned, 0.0)
        tab[pl.ds(8 + rows + leaves, ghosts), :] = jnp.where(low, 0.0, turned)
        tab[pl.ds(8 + rows + leaves + ghosts, ghosts), :] = jnp.where(low, 0.0, got)
        copy.wait()

    now = lax.rem(step, 2) * (PAIRS * PITCH)
    before = lax.rem(step + 1, 2) * (PAIRS * PITCH)
    lane_of = lax.broadcasted_iota(jnp.int32, (8, 128), 0)

    def collect(cells, slots):
        lines = [src_ref.at[pl.ds(cell * SLOTS, SLOTS)] for cell in cells]
        for pack in range(SLOTS // 16):
            parts = [[] for _ in cells]
            for start in (pack * 16, pack * 16 + 8):
                totals = [None] * len(cells)
                for j in range(min(8, inter - start)):
                    for u, line in enumerate(lines):
                        window = tab[pl.ds(line[start + j], 8), :]
                        totals[u] = window if j == 0 else jnp.where(lane_of == j, window, totals[u])
                for u in range(len(cells)):
                    parts[u].append(totals[u])
            for u, slot in enumerate(slots):
                held[slot, pl.ds(pack * 16, 16), :] = jnp.concatenate(parts[u], axis=0).astype(jnp.bfloat16)

    def pick(cell, rows_of):
        line = jnp.broadcast_to(off_ref[pl.ds(cell, 1), :], (16, 256)).astype(jnp.bfloat16)
        line = jnp.concatenate([line] * (PAIRS // 16), axis=0)
        chosen = jnp.where(iota[...] == line, jnp.bfloat16(1), jnp.bfloat16(0))
        return jnp.dot(chosen[:, :SLOTS], rows_of, preferred_element_type=jnp.float32)

    def contract(tile, count):
        pieces = []
        for t in range(2 * count):
            at = before + (2 * tile + t) * PITCH
            pieces.append(placed[pl.ds(at, GROUP), :].astype(jnp.bfloat16))
        both = jnp.concatenate(pieces, axis=1)
        kern = m2l_ref[:, pl.ds(pl.multiple_of(tile * 256, 256), 256 * count)]
        return lax.dot_general(both, kern, (((1,), (1,)), ((), ())), preferred_element_type=jnp.float32)

    out_ref[...] = jnp.zeros_like(out_ref)

    @pl.when(step < last)
    def _():
        def body(it, carry):
            cell = UNROLL * it
            part = contract(cell, UNROLL)
            olds = [held[u] for u in range(UNROLL)]
            results = []
            for u in range(UNROLL):
                back = jnp.where(it == 0, GROUP - UNROLL, cell - UNROLL) + u
                results.append((back, pick(back, olds[u])))
            collect([cell + u for u in range(UNROLL)], list(range(UNROLL)))
            for back, result in results:
                placed[pl.ds(now + back, PAIRS, stride=PITCH), :] = result
            out_ref[...] += part
            return carry
        lax.fori_loop(0, GROUP // UNROLL, body, 0)
        for u in range(UNROLL):
            back = GROUP - UNROLL + u
            placed[pl.ds(now + back, PAIRS, stride=PITCH), :] = pick(back, held[u])

    @pl.when(step == last)
    def _():
        def body(it, carry):
            out_ref[...] += contract(it * UNROLL, UNROLL)
            return carry
        lax.fori_loop(0, GROUP // UNROLL, body, 0)


def translate(own, ghost, sources, offsets, m2l_kernels):
    leaves, inter = sources.shape
    ghosts = ghost.shape[0]
    rows = leaves + 2 * ghosts
    remote = sources - leaves
    row = jnp.where(remote < 0, sources, leaves + lax.shift_right_arithmetic(remote, 1) + (remote & 1) * ghosts)
    row = row + (offsets & 1) * rows
    row = row + 8 - jnp.arange(inter, dtype=jnp.int32)[None, :] % 8
    row = jnp.pad(row, ((0, 0), (0, SLOTS - inter))).reshape(-1)
    pair = jnp.pad((offsets >> 1).astype(jnp.float32), ((0, 0), (0, 256 - inter)), constant_values=-1.0)
    steps = leaves // GROUP
    return pl.pallas_call(
        functools.partial(translate_kernel, leaves, inter),
        grid=(steps + 1,),
        in_specs=[
            pl.BlockSpec((GROUP * SLOTS,), lambda i: (jnp.minimum(i, steps - 1),), memory_space=pltpu.SMEM),
            pl.BlockSpec((GROUP, 256), lambda i: (jnp.minimum(i, steps - 1), 0)),
            pl.BlockSpec(own.shape, lambda i: (0, 0)),
            pl.BlockSpec(ghost.shape, lambda i: (0, 0)),
            pl.BlockSpec(memory_space=pl.ANY),
        ],
        out_specs=pl.BlockSpec((GROUP, 64), lambda i: (jnp.maximum(i - 1, 0), 0)),
        out_shape=jax.ShapeDtypeStruct((leaves, 64), jnp.float32),
        scratch_shapes=[
            pltpu.VMEM((2 * rows + 16, 128), jnp.float32),
            pltpu.VMEM((PAIRS, 256), jnp.bfloat16),
            pltpu.VMEM((UNROLL, SLOTS, 128), jnp.bfloat16),
            pltpu.VMEM((2 * PAIRS * PITCH, 128), jnp.float32),
            pltpu.VMEM((RANK, PAIRS * 128), jnp.bfloat16),
            pltpu.SemaphoreType.DMA,
        ],
        compiler_params=params(),
    )(row, pair, own, ghost, m2l_kernels)


def evaluate_kernel(turned_ref, leaf_ref, local_ref, expand_ref, out_ref, nodes, result):
    step = pl.program_id(0)
    leaves = local_ref.shape[0]

    @pl.when(step == 0)
    def _():
        local = jnp.concatenate([part.astype(jnp.float32) for part in split_two(local_ref[...])], axis=1)
        local = local.T.astype(jnp.bfloat16)
        large, small = split_two(expand_ref[...])
        expands = jnp.concatenate([large, large, small], axis=1)
        width = 2 * REGION
        for pair in range(nodes.shape[0] // 2):
            ids = leaf_ref[:, pl.ds(pair * width, width)]
            onehot = lax.broadcasted_iota(jnp.int32, (leaves, width), 0) == ids
            onehot = jnp.where(onehot, 1.0, 0.0).astype(jnp.bfloat16)
            picked = jnp.dot(local, onehot, preferred_element_type=jnp.float32).astype(jnp.bfloat16)
            terms = jnp.concatenate([picked, picked[:RANK]], axis=0)
            values = jnp.dot(expands, terms, preferred_element_type=jnp.float32)
            nodes[2 * pair] = values[:, :REGION]
            nodes[2 * pair + 1] = values[:, REGION:]

    def chunk(v, carry):
        at = pl.ds(pl.multiple_of(v * 16, 16), 16)
        px, py, pz = (chebyshev(turned_ref[dim, at, :]) for dim in range(3))
        value = None
        for i in range(ORDER):
            middle = None
            for j in range(ORDER):
                first = (i * ORDER + j) * ORDER
                inner = nodes[step, pl.ds(first + 1, 1), :] * pz[0] + nodes[step, pl.ds(first, 1), :]
                for k in range(2, ORDER):
                    inner += nodes[step, pl.ds(first + k, 1), :] * pz[k - 1]
                middle = inner if j == 0 else middle + inner * py[j - 1]
            value = middle if i == 0 else value + middle * px[i - 1]
        result[at, :] = value
        return carry

    lax.fori_loop(0, BLOCK // 16, chunk, 0)
    out_ref[...] = result[...].T


def on_device(
    coords,
    masses,
    swap_counts,
    leaf_of_block,
    let_send,
    inter_source,
    inter_offset,
    compress,
    m2l_kernels,
    expand,
):
    nodes_count = compress.shape[0]
    leaves = inter_source.shape[0]
    local_bodies = coords.shape[1]
    blocks = local_bodies // BLOCK
    regions = blocks // REGION
    peers, per_peer = let_send.shape[1:]
    coords = coords.reshape(3, blocks, BLOCK)
    masses = masses.reshape(blocks, BLOCK)
    hbm = pl.BlockSpec(memory_space=pl.ANY)
    coords_block, masses_block = (3, REGION, BLOCK), (REGION, BLOCK)

    def region_of(g):
        return lax.rem(g + SWAPS, regions)

    sums, turned = pl.pallas_call(
        moments_kernel,
        grid=(regions,),
        in_specs=[
            pl.BlockSpec(memory_space=pltpu.SMEM),
            pl.BlockSpec(coords_block, lambda g: (0, region_of(g), 0)),
            pl.BlockSpec(masses_block, lambda g: (region_of(g), 0)),
            hbm,
            hbm,
        ],
        out_specs=[
            pl.BlockSpec((nodes_count, REGION), lambda g: (0, region_of(g))),
            pl.BlockSpec((3, BLOCK, REGION), lambda g: (0, 0, region_of(g))),
        ],
        out_shape=[
            jax.ShapeDtypeStruct((nodes_count, blocks), jnp.float32),
            jax.ShapeDtypeStruct((3, BLOCK, blocks), jnp.float32),
        ],
        scratch_shapes=[
            pltpu.VMEM(coords_block, jnp.float32),
            pltpu.VMEM(masses_block, jnp.float32),
            pltpu.VMEM((SWAPS, 4, REGION, BLOCK), jnp.float32),
            pltpu.SemaphoreType.DMA((2 * SWAPS,)),
            pltpu.SemaphoreType.DMA((2 * SWAPS,)),
        ]
        + moment_scratch(nodes_count),
        compiler_params=params(collective_id=1, has_side_effects=True),
    )(swap_counts.reshape(SWAPS), coords, masses, coords, masses)
    basis = node_basis()
    exact = functools.partial(jnp.dot, precision=lax.Precision.HIGHEST, preferred_element_type=jnp.float32)
    compress_polys = exact(compress.T, basis)
    expand_polys = exact(basis.T, expand.T)
    leaf_row = leaf_of_block.reshape(1, blocks)
    send = let_send.reshape(peers, per_peer) + 8 - (jnp.arange(per_peer, dtype=jnp.int32)[None, :] // 2) % 8
    vmem = pl.BlockSpec(memory_space=pltpu.VMEM)
    own, incoming = pl.pallas_call(
        coefficients_kernel,
        in_specs=[pl.BlockSpec(memory_space=pltpu.SMEM), vmem, vmem, vmem],
        out_specs=[vmem, vmem],
        out_shape=[
            jax.ShapeDtypeStruct((leaves, 2 * RANK), jnp.float32),
            jax.ShapeDtypeStruct((peers * per_peer // 2, 2 * RANK), jnp.bfloat16),
        ],
        scratch_shapes=[
            pltpu.VMEM((leaves + 16, 2 * RANK), jnp.float32),
            pltpu.VMEM((peers * per_peer // 2, 2 * RANK), jnp.bfloat16),
            pltpu.SemaphoreType.DMA,
            pltpu.SemaphoreType.DMA,
        ],
        compiler_params=params(collective_id=0, has_side_effects=True),
    )(send.reshape(-1), sums, leaf_row, compress_polys)
    local = translate(own, incoming, inter_source, inter_offset, m2l_kernels)
    values = pl.pallas_call(
        evaluate_kernel,
        grid=(regions,),
        in_specs=[
            pl.BlockSpec((3, BLOCK, REGION), lambda g: (0, 0, g)),
            pl.BlockSpec((1, blocks), lambda g: (0, 0)),
            pl.BlockSpec((leaves, RANK), lambda g: (0, 0)),
            pl.BlockSpec((nodes_count, RANK), lambda g: (0, 0)),
        ],
        out_specs=pl.BlockSpec((REGION, BLOCK), lambda g: (g, 0)),
        out_shape=jax.ShapeDtypeStruct((blocks, BLOCK), jnp.float32),
        scratch_shapes=[
            pltpu.VMEM((regions, nodes_count, REGION), jnp.float32),
            pltpu.VMEM((BLOCK, REGION), jnp.float32),
        ],
        compiler_params=params(),
    )(turned, leaf_row, local, expand_polys)
    return values.reshape(local_bodies)


def solution(mesh):
    return jax.shard_map(
        on_device,
        mesh=mesh,
        in_specs=(
            P(None, ("space", "sub")),
            P(("space", "sub")),
            P(("space", "sub"), None),
            P(("space", "sub")),
            P(("space", "sub"), None, None),
            P(("space", "sub"), None),
            P(("space", "sub"), None),
            P(),
            P(),
            P(),
        ),
        out_specs=P(("space", "sub")),
        check_vma=False,
    )
```

```python
import functools

import jax
import jax.numpy as jnp
import numpy as np
from jax import lax
from jax.experimental import pallas as pl
from jax.experimental.pallas import tpu as pltpu
from jax.sharding import PartitionSpec as P

ORDER = 6
RANK = 64
BLOCK = 128
REGION = 128
SWAPS = 3
GROUP = 80
SLOTS = 192
PAIRS = 160
PITCH = 81
UNROLL = 8
STRIDE = 9
BATCH = 4


def params(**more):
    return pltpu.CompilerParams(vmem_limit_bytes=56 << 20, **more)


def chebyshev(points):
    twice = 2.0 * points
    polys = [points, twice * points - 1.0]
    for _ in range(ORDER - 3):
        polys.append(twice * polys[-1] - polys[-2])
    return polys


def node_basis():
    single = np.zeros((ORDER, ORDER))
    for j in range(ORDER):
        for k in range(ORDER):
            single[j, k] = np.cos(k * (2 * j + 1) * np.pi / (2 * ORDER)) * (1.0 if k == 0 else 2.0) / ORDER
    return np.kron(np.kron(single, single), single).astype(np.float32)


def split_two(values):
    first = values.astype(jnp.bfloat16)
    return first, (values - first.astype(jnp.float32)).astype(jnp.bfloat16)


def gather_moments(coords, masses, out_ref, turned_ref, px, py, pz, partial):
    mass = masses[...].T
    px[0] = mass
    for dim, scratch in enumerate((px, py, pz)):
        points = coords[dim].T
        turned_ref[dim] = points
        for k, poly in enumerate(chebyshev(points)):
            scratch[k + 1] = poly * mass if dim == 0 else poly

    def along(i, carry):
        def chunk(v, sums):
            at = pl.ds(pl.multiple_of(v * 8, 8), 8)
            left = px[i, at, :]
            inner = [pz[k, at, :] for k in range(1, ORDER)]
            new = []
            for j in range(ORDER):
                pair = left if j == 0 else left * py[j, at, :]
                new.append(sums[j * ORDER] + pair)
                for k in range(1, ORDER):
                    new.append(sums[j * ORDER + k] + pair * inner[k - 1])
            return tuple(new)

        zero = jnp.zeros((8, REGION), jnp.float32)
        sums = lax.fori_loop(0, BLOCK // 8, chunk, (zero,) * (ORDER * ORDER), unroll=4)
        for n in range(ORDER * ORDER):
            partial[pl.ds((i * ORDER * ORDER + n) * STRIDE, 8), :] = sums[n]
        return carry

    lax.fori_loop(0, ORDER, along, 0)
    count = out_ref.shape[0]
    total = partial[pl.ds(0, count, stride=STRIDE), :]
    for s in range(1, 8):
        total += partial[pl.ds(s, count, stride=STRIDE), :]
    out_ref[...] = total


def moments_kernel(
    counts_ref,
    coords_ref,
    masses_ref,
    all_coords,
    all_masses,
    out_ref,
    turned_ref,
    coords,
    masses,
    got,
    send_sem,
    recv_sem,
    px,
    py,
    pz,
    partial,
):
    step = pl.program_id(0)
    stays = pl.num_programs(0) - SWAPS
    space, sub = lax.axis_index("space"), lax.axis_index("sub")
    spaces = lax.axis_size("space")
    partners = (
        (lax.rem(space + spaces // 2, spaces), sub),
        (space + 1 - 2 * lax.rem(space, 2), sub),
        (space, sub + 1 - 2 * lax.rem(sub, 2)),
    )
    column = lax.broadcasted_iota(jnp.int32, (REGION, BLOCK), 0) * BLOCK + lax.broadcasted_iota(
        jnp.int32, (REGION, BLOCK), 1
    )

    def copies(rnd):
        at = pl.ds(rnd * REGION, REGION)
        pairs = ((all_coords.at[:, at, :], got.at[rnd, pl.ds(0, 3)]), (all_masses.at[at, :], got.at[rnd, 3]))
        return [
            pltpu.make_async_remote_copy(
                src_ref=source,
                dst_ref=target,
                send_sem=send_sem.at[2 * rnd + k],
                recv_sem=recv_sem.at[2 * rnd + k],
                device_id=partners[rnd],
                device_id_type=pl.DeviceIdType.MESH,
            )
            for k, (source, target) in enumerate(pairs)
        ]

    @pl.when(step == 0)
    def _():
        barrier = pltpu.get_barrier_semaphore()
        for partner in partners:
            pl.semaphore_signal(barrier, inc=1, device_id=partner, device_id_type=pl.DeviceIdType.MESH)
        pl.semaphore_wait(barrier, SWAPS)
        for rnd in range(SWAPS):
            for copy in copies(rnd):
                copy.start()

    @pl.when(step < stays)
    def _():
        coords[...] = coords_ref[...]
        masses[...] = masses_ref[...]

    for rnd in range(SWAPS):

        @pl.when(step == stays + rnd)
        def _():
            for copy in copies(rnd):
                copy.wait_recv()
            keep = column < counts_ref[rnd]
            for dim in range(3):
                coords[dim] = jnp.where(keep, got[rnd, dim], coords_ref[dim])
            masses[...] = jnp.where(keep, got[rnd, 3], masses_ref[...])

    gather_moments(coords, masses, out_ref, turned_ref, px, py, pz, partial)

    @pl.when(step == stays + SWAPS - 1)
    def _():
        for rnd in range(SWAPS):
            for copy in copies(rnd):
                copy.wait_send()


def moment_scratch(nodes_count):
    return [pltpu.VMEM((ORDER, BLOCK, REGION), jnp.float32) for _ in range(3)] + [
        pltpu.VMEM((STRIDE * nodes_count, REGION), jnp.float32)
    ]


def coefficients_kernel(
    send_ref,
    sums_ref,
    leaf_ref,
    compress_ref,
    expand_ref,
    basis_ref,
    source_ref,
    offset_ref,
    own_ref,
    got_ref,
    polys_ref,
    row_ref,
    pair_ref,
    padded,
    packed,
    send_sem,
    recv_sem,
):
    leaves = own_ref.shape[0]
    peers = got_ref.shape[0] // 16
    subs = lax.axis_size("sub")
    me = lax.axis_index("space") * subs + lax.axis_index("sub")
    barrier = pltpu.get_barrier_semaphore()

    def greet(hop, carry):
        peer = lax.rem(me + hop, peers)
        pl.semaphore_signal(
            barrier, inc=1, device_id=(peer // subs, lax.rem(peer, subs)), device_id_type=pl.DeviceIdType.MESH
        )
        return carry

    lax.fori_loop(1, peers, greet, 0)
    onehot = lax.broadcasted_iota(jnp.int32, (leaves, leaf_ref.shape[1]), 0) == leaf_ref[...]
    onehot = jnp.where(onehot, 1.0, 0.0).astype(jnp.bfloat16)
    exact = functools.partial(
        lax.dot_general, precision=lax.Precision.HIGHEST, preferred_element_type=jnp.float32
    )
    compress = exact(compress_ref[...], basis_ref[...], (((1,), (0,)), ((), ())))
    moved = exact(compress, sums_ref[...], (((1,), (0,)), ((), ())))
    both = jnp.concatenate(split_two(moved), axis=0)
    total = lax.dot_general(onehot, both, (((1,), (1,)), ((), ())), preferred_element_type=jnp.float32)
    own = (total + pltpu.roll(total, RANK, 1)).astype(jnp.bfloat16).astype(jnp.float32)
    own_ref[...] = own
    padded[pl.ds(0, 8), :] = jnp.zeros((8, 2 * RANK), jnp.float32)
    padded[pl.ds(8, leaves), :] = own
    padded[pl.ds(8 + leaves, 8), :] = jnp.zeros((8, 2 * RANK), jnp.float32)
    row_of = lax.broadcasted_iota(jnp.int32, (8, 2 * RANK), 0)
    low = lax.broadcasted_iota(jnp.int32, (8, 2 * RANK), 1) < RANK

    def pack(peer):
        line = send_ref.at[pl.ds(peer * 32, 32)]
        halves = []
        for start in (0, 8):
            rows = None
            for j in range(8):
                slot = 2 * (start + j)
                both = jnp.where(low, padded[pl.ds(line[slot], 8), :], padded[pl.ds(line[slot + 1], 8), :])
                rows = both if rows is None else jnp.where(row_of == j, both, rows)
            halves.append(rows)
        return jnp.concatenate(halves, axis=0).astype(jnp.bfloat16)

    def send(hops):
        rows = [lax.rem(me + hop, peers) for hop in hops]
        for peer in rows:
            packed[pl.ds(pl.multiple_of(peer * 16, 16), 16), :] = pack(peer)
        for peer in rows:
            pltpu.make_async_remote_copy(
                src_ref=packed.at[pl.ds(pl.multiple_of(peer * 16, 16), 16), :],
                dst_ref=got_ref.at[mine, :],
                send_sem=send_sem,
                recv_sem=recv_sem,
                device_id=(peer // subs, lax.rem(peer, subs)),
                device_id_type=pl.DeviceIdType.MESH,
            ).start()

    def send_batch(batch, carry):
        send([1 + batch * BATCH + k for k in range(BATCH)])
        return carry

    mine = pl.ds(pl.multiple_of(me * 16, 16), 16)
    got_ref[mine, :] = pack(me)
    pl.semaphore_wait(barrier, peers - 1)
    batches = (peers - 1) // BATCH
    lax.fori_loop(0, batches, send_batch, 0)
    if batches * BATCH < peers - 1:
        send(range(1 + batches * BATCH, peers))

    polys_ref[...] = exact(basis_ref[...], expand_ref[...], (((0,), (0,)), ((), ())))
    inter = source_ref.shape[1]
    ghosts = got_ref.shape[0]
    rows = leaves + 2 * ghosts
    sources, offsets = source_ref[...], offset_ref[...]
    remote = sources - leaves
    row = leaves + lax.shift_right_arithmetic(remote, 1) + (remote & 1) * ghosts
    row = jnp.where(remote < 0, sources, row) + (offsets & 1) * rows
    row_ref[...] = jnp.zeros_like(row_ref)
    row_ref[:, :inter] = row + 8 - lax.rem(lax.broadcasted_iota(jnp.int32, row.shape, 1), 8)
    pair_ref[...] = jnp.full_like(pair_ref, -1.0)
    pair_ref[:, :inter] = lax.shift_right_arithmetic(offsets, 1).astype(jnp.float32)

    others = pl.ds(0, (peers - 1) * 16)
    everything = pltpu.make_async_remote_copy(
        src_ref=packed.at[others, :],
        dst_ref=got_ref.at[others, :],
        send_sem=send_sem,
        recv_sem=recv_sem,
        device_id=(lax.axis_index("space"), lax.axis_index("sub")),
        device_id_type=pl.DeviceIdType.MESH,
    )
    everything.wait_send()
    everything.wait_recv()


def translate_kernel(leaves, inter, src_ref, off_ref, own_ref, ghost_ref, kernels_ref, out_ref, tab, iota, held, placed, m2l_ref, sem):
    step = pl.program_id(0)
    last = pl.num_programs(0) - 1
    rows = (tab.shape[0] - 16) // 2
    ghosts = ghost_ref.shape[0]

    @pl.when(step == 0)
    def _():
        width = kernels_ref.shape[1]
        copy = pltpu.make_async_copy(kernels_ref, m2l_ref.at[:, pl.ds(0, width)], sem)
        copy.start()
        m2l_ref[:, pl.ds(width, m2l_ref.shape[1] - width)] = jnp.zeros(
            (m2l_ref.shape[0], m2l_ref.shape[1] - width), jnp.bfloat16
        )
        iota[...] = lax.broadcasted_iota(jnp.int32, iota.shape, 0).astype(jnp.float32).astype(jnp.bfloat16)
        held[...] = jnp.zeros_like(held)
        tab[pl.ds(0, 8), :] = jnp.zeros((8, 128), jnp.float32)
        tab[pl.ds(2 * rows + 8, 8), :] = jnp.zeros((8, 128), jnp.float32)
        low = lax.broadcasted_iota(jnp.int32, (leaves, 128), 1) < 64
        own = own_ref[...]
        tab[pl.ds(8, leaves), :] = jnp.where(low, own, 0.0)
        tab[pl.ds(8 + rows, leaves), :] = jnp.where(low, 0.0, own)
        low = lax.broadcasted_iota(jnp.int32, (ghosts, 128), 1) < 64
        got = ghost_ref[...].astype(jnp.float32)
        turned = pltpu.roll(got, 64, 1)
        tab[pl.ds(8 + leaves, ghosts), :] = jnp.where(low, got, 0.0)
        tab[pl.ds(8 + leaves + ghosts, ghosts), :] = jnp.where(low, turned, 0.0)
        tab[pl.ds(8 + rows + leaves, ghosts), :] = jnp.where(low, 0.0, turned)
        tab[pl.ds(8 + rows + leaves + ghosts, ghosts), :] = jnp.where(low, 0.0, got)
        copy.wait()

    now = lax.rem(step, 2) * (PAIRS * PITCH)
    before = lax.rem(step + 1, 2) * (PAIRS * PITCH)
    lane_of = lax.broadcasted_iota(jnp.int32, (8, 128), 0)

    def collect(cells, slots):
        lines = [src_ref.at[pl.ds(cell * SLOTS, SLOTS)] for cell in cells]
        for pack in range(SLOTS // 16):
            parts = [[] for _ in cells]
            for start in (pack * 16, pack * 16 + 8):
                totals = [None] * len(cells)
                for j in range(min(8, inter - start)):
                    for u, line in enumerate(lines):
                        window = tab[pl.ds(line[start + j], 8), :]
                        totals[u] = window if j == 0 else jnp.where(lane_of == j, window, totals[u])
                for u in range(len(cells)):
                    parts[u].append(totals[u])
            for u, slot in enumerate(slots):
                held[slot, pl.ds(pack * 16, 16), :] = jnp.concatenate(parts[u], axis=0).astype(jnp.bfloat16)

    def pick(cell, rows_of):
        line = jnp.broadcast_to(off_ref[pl.ds(cell, 1), :], (16, 256)).astype(jnp.bfloat16)
        line = jnp.concatenate([line] * (PAIRS // 16), axis=0)
        chosen = jnp.where(iota[...] == line, jnp.bfloat16(1), jnp.bfloat16(0))
        return jnp.dot(chosen[:, :SLOTS], rows_of, preferred_element_type=jnp.float32)

    def contract(tile, count):
        pieces = []
        for t in range(2 * count):
            at = before + (2 * tile + t) * PITCH
            pieces.append(placed[pl.ds(at, GROUP), :].astype(jnp.bfloat16))
        both = jnp.concatenate(pieces, axis=1)
        kern = m2l_ref[:, pl.ds(pl.multiple_of(tile * 256, 256), 256 * count)]
        return lax.dot_general(both, kern, (((1,), (1,)), ((), ())), preferred_element_type=jnp.float32)

    out_ref[...] = jnp.zeros_like(out_ref)

    @pl.when(step < last)
    def _():
        def body(it, carry):
            cell = UNROLL * it
            part = contract(cell, UNROLL)
            olds = [held[u] for u in range(UNROLL)]
            results = []
            for u in range(UNROLL):
                back = jnp.where(it == 0, GROUP - UNROLL, cell - UNROLL) + u
                results.append((back, pick(back, olds[u])))
            collect([cell + u for u in range(UNROLL)], list(range(UNROLL)))
            for back, result in results:
                placed[pl.ds(now + back, PAIRS, stride=PITCH), :] = result
            out_ref[...] += part
            return carry
        lax.fori_loop(0, GROUP // UNROLL, body, 0)
        for u in range(UNROLL):
            back = GROUP - UNROLL + u
            placed[pl.ds(now + back, PAIRS, stride=PITCH), :] = pick(back, held[u])

    @pl.when(step == last)
    def _():
        def body(it, carry):
            out_ref[...] += contract(it * UNROLL, UNROLL)
            return carry
        lax.fori_loop(0, GROUP // UNROLL, body, 0)


def translate(own, ghost, row, pair, inter, m2l_kernels):
    leaves = own.shape[0]
    ghosts = ghost.shape[0]
    rows = leaves + 2 * ghosts
    steps = leaves // GROUP
    return pl.pallas_call(
        functools.partial(translate_kernel, leaves, inter),
        grid=(steps + 1,),
        in_specs=[
            pl.BlockSpec((GROUP * SLOTS,), lambda i: (jnp.minimum(i, steps - 1),), memory_space=pltpu.SMEM),
            pl.BlockSpec((GROUP, 256), lambda i: (jnp.minimum(i, steps - 1), 0)),
            pl.BlockSpec(own.shape, lambda i: (0, 0)),
            pl.BlockSpec(ghost.shape, lambda i: (0, 0)),
            pl.BlockSpec(memory_space=pl.ANY),
        ],
        out_specs=pl.BlockSpec((GROUP, 64), lambda i: (jnp.maximum(i - 1, 0), 0)),
        out_shape=jax.ShapeDtypeStruct((leaves, 64), jnp.float32),
        scratch_shapes=[
            pltpu.VMEM((2 * rows + 16, 128), jnp.float32),
            pltpu.VMEM((PAIRS, 256), jnp.bfloat16),
            pltpu.VMEM((UNROLL, SLOTS, 128), jnp.bfloat16),
            pltpu.VMEM((2 * PAIRS * PITCH, 128), jnp.float32),
            pltpu.VMEM((RANK, PAIRS * 128), jnp.bfloat16),
            pltpu.SemaphoreType.DMA,
        ],
        compiler_params=params(),
    )(row.reshape(-1), pair, own, ghost, m2l_kernels)


def evaluate_kernel(turned_ref, leaf_ref, local_ref, expand_ref, out_ref, nodes, result):
    step = pl.program_id(0)
    leaves = local_ref.shape[0]

    @pl.when(step == 0)
    def _():
        local = jnp.concatenate([part.astype(jnp.float32) for part in split_two(local_ref[...])], axis=1)
        local = local.T.astype(jnp.bfloat16)
        large, small = split_two(expand_ref[...])
        expands = jnp.concatenate([large, large, small], axis=1)
        width = 2 * REGION
        for pair in range(nodes.shape[0] // 2):
            ids = leaf_ref[:, pl.ds(pair * width, width)]
            onehot = lax.broadcasted_iota(jnp.int32, (leaves, width), 0) == ids
            onehot = jnp.where(onehot, 1.0, 0.0).astype(jnp.bfloat16)
            picked = jnp.dot(local, onehot, preferred_element_type=jnp.float32).astype(jnp.bfloat16)
            terms = jnp.concatenate([picked, picked[:RANK]], axis=0)
            values = jnp.dot(expands, terms, preferred_element_type=jnp.float32)
            nodes[2 * pair] = values[:, :REGION]
            nodes[2 * pair + 1] = values[:, REGION:]

    def chunk(v, carry):
        at = pl.ds(pl.multiple_of(v * 16, 16), 16)
        px, py, pz = (chebyshev(turned_ref[dim, at, :]) for dim in range(3))
        value = None
        for i in range(ORDER):
            middle = None
            for j in range(ORDER):
                first = (i * ORDER + j) * ORDER
                inner = nodes[step, pl.ds(first + 1, 1), :] * pz[0] + nodes[step, pl.ds(first, 1), :]
                for k in range(2, ORDER):
                    inner += nodes[step, pl.ds(first + k, 1), :] * pz[k - 1]
                middle = inner if j == 0 else middle + inner * py[j - 1]
            value = middle if i == 0 else value + middle * px[i - 1]
        result[at, :] = value
        return carry

    lax.fori_loop(0, BLOCK // 16, chunk, 0)
    out_ref[...] = result[...].T


def on_device(
    coords,
    masses,
    swap_counts,
    leaf_of_block,
    let_send,
    inter_source,
    inter_offset,
    compress,
    m2l_kernels,
    expand,
):
    nodes_count = compress.shape[0]
    leaves = inter_source.shape[0]
    local_bodies = coords.shape[1]
    blocks = local_bodies // BLOCK
    regions = blocks // REGION
    peers, per_peer = let_send.shape[1:]
    coords = coords.reshape(3, blocks, BLOCK)
    masses = masses.reshape(blocks, BLOCK)
    hbm = pl.BlockSpec(memory_space=pl.ANY)
    coords_block, masses_block = (3, REGION, BLOCK), (REGION, BLOCK)

    def region_of(g):
        return lax.rem(g + SWAPS, regions)

    sums, turned = pl.pallas_call(
        moments_kernel,
        grid=(regions,),
        in_specs=[
            pl.BlockSpec(memory_space=pltpu.SMEM),
            pl.BlockSpec(coords_block, lambda g: (0, region_of(g), 0)),
            pl.BlockSpec(masses_block, lambda g: (region_of(g), 0)),
            hbm,
            hbm,
        ],
        out_specs=[
            pl.BlockSpec((nodes_count, REGION), lambda g: (0, region_of(g))),
            pl.BlockSpec((3, BLOCK, REGION), lambda g: (0, 0, region_of(g))),
        ],
        out_shape=[
            jax.ShapeDtypeStruct((nodes_count, blocks), jnp.float32),
            jax.ShapeDtypeStruct((3, BLOCK, blocks), jnp.float32),
        ],
        scratch_shapes=[
            pltpu.VMEM(coords_block, jnp.float32),
            pltpu.VMEM(masses_block, jnp.float32),
            pltpu.VMEM((SWAPS, 4, REGION, BLOCK), jnp.float32),
            pltpu.SemaphoreType.DMA((2 * SWAPS,)),
            pltpu.SemaphoreType.DMA((2 * SWAPS,)),
        ]
        + moment_scratch(nodes_count),
        compiler_params=params(collective_id=1, has_side_effects=True),
    )(swap_counts.reshape(SWAPS), coords, masses, coords, masses)
    leaf_row = leaf_of_block.reshape(1, blocks)
    send = let_send.reshape(peers, per_peer) + 8 - (jnp.arange(per_peer, dtype=jnp.int32)[None, :] // 2) % 8
    vmem = pl.BlockSpec(memory_space=pltpu.VMEM)
    own, incoming, expand_polys, row, pair = pl.pallas_call(
        coefficients_kernel,
        in_specs=[pl.BlockSpec(memory_space=pltpu.SMEM)] + [vmem] * 7,
        out_specs=[vmem] * 5,
        out_shape=[
            jax.ShapeDtypeStruct((leaves, 2 * RANK), jnp.float32),
            jax.ShapeDtypeStruct((peers * per_peer // 2, 2 * RANK), jnp.bfloat16),
            jax.ShapeDtypeStruct((nodes_count, RANK), jnp.float32),
            jax.ShapeDtypeStruct((leaves, SLOTS), jnp.int32),
            jax.ShapeDtypeStruct((leaves, 256), jnp.float32),
        ],
        scratch_shapes=[
            pltpu.VMEM((leaves + 16, 2 * RANK), jnp.float32),
            pltpu.VMEM((peers * per_peer // 2, 2 * RANK), jnp.bfloat16),
            pltpu.SemaphoreType.DMA,
            pltpu.SemaphoreType.DMA,
        ],
        compiler_params=params(collective_id=0, has_side_effects=True),
    )(send.reshape(-1), sums, leaf_row, compress.T, expand.T, node_basis(), inter_source, inter_offset)
    local = translate(own, incoming, row, pair, inter_source.shape[1], m2l_kernels)
    values = pl.pallas_call(
        evaluate_kernel,
        grid=(regions,),
        in_specs=[
            pl.BlockSpec((3, BLOCK, REGION), lambda g: (0, 0, g)),
            pl.BlockSpec((1, blocks), lambda g: (0, 0)),
            pl.BlockSpec((leaves, RANK), lambda g: (0, 0)),
            pl.BlockSpec((nodes_count, RANK), lambda g: (0, 0)),
        ],
        out_specs=pl.BlockSpec((REGION, BLOCK), lambda g: (g, 0)),
        out_shape=jax.ShapeDtypeStruct((blocks, BLOCK), jnp.float32),
        scratch_shapes=[
            pltpu.VMEM((regions, nodes_count, REGION), jnp.float32),
            pltpu.VMEM((BLOCK, REGION), jnp.float32),
        ],
        compiler_params=params(),
    )(turned, leaf_row, local, expand_polys)
    return values.reshape(local_bodies)


def solution(mesh):
    return jax.shard_map(
        on_device,
        mesh=mesh,
        in_specs=(
            P(None, ("space", "sub")),
            P(("space", "sub")),
            P(("space", "sub"), None),
            P(("space", "sub")),
            P(("space", "sub"), None, None),
            P(("space", "sub"), None),
            P(("space", "sub"), None),
            P(),
            P(),
            P(),
        ),
        out_specs=P(("space", "sub")),
        check_vma=False,
    )
```

```python
import functools

import jax
import jax.numpy as jnp
import numpy as np
from jax import lax
from jax.experimental import pallas as pl
from jax.experimental.pallas import tpu as pltpu
from jax.sharding import PartitionSpec as P

ORDER = 6
RANK = 64
BLOCK = 128
REGION = 128
SWAPS = 3
GROUP = 80
SLOTS = 192
PAIRS = 160
PITCH = 81
UNROLL = 8
STRIDE = 9
BATCH = 4


def params(**more):
    return pltpu.CompilerParams(vmem_limit_bytes=56 << 20, **more)


def chebyshev(points):
    twice = 2.0 * points
    polys = [points, twice * points - 1.0]
    for _ in range(ORDER - 3):
        polys.append(twice * polys[-1] - polys[-2])
    return polys


def node_basis():
    single = np.zeros((ORDER, ORDER))
    for j in range(ORDER):
        for k in range(ORDER):
            single[j, k] = np.cos(k * (2 * j + 1) * np.pi / (2 * ORDER)) * (1.0 if k == 0 else 2.0) / ORDER
    return np.kron(np.kron(single, single), single).astype(np.float32)


def split_two(values):
    first = values.astype(jnp.bfloat16)
    return first, (values - first.astype(jnp.float32)).astype(jnp.bfloat16)


def gather_moments(coords, masses, out_ref, turned_ref, px, py, pz, partial):
    mass = masses[...].T
    px[0] = mass
    for dim, scratch in enumerate((px, py, pz)):
        points = coords[dim].T
        turned_ref[dim] = points
        for k, poly in enumerate(chebyshev(points)):
            scratch[k + 1] = poly * mass if dim == 0 else poly

    def along(i, carry):
        def chunk(v, sums):
            at = pl.ds(pl.multiple_of(v * 8, 8), 8)
            left = px[i, at, :]
            inner = [pz[k, at, :] for k in range(1, ORDER)]
            new = []
            for j in range(ORDER):
                pair = left if j == 0 else left * py[j, at, :]
                new.append(sums[j * ORDER] + pair)
                for k in range(1, ORDER):
                    new.append(sums[j * ORDER + k] + pair * inner[k - 1])
            return tuple(new)

        zero = jnp.zeros((8, REGION), jnp.float32)
        sums = lax.fori_loop(0, BLOCK // 8, chunk, (zero,) * (ORDER * ORDER), unroll=4)
        for n in range(ORDER * ORDER):
            partial[pl.ds((i * ORDER * ORDER + n) * STRIDE, 8), :] = sums[n]
        return carry

    lax.fori_loop(0, ORDER, along, 0)
    count = out_ref.shape[0]
    total = partial[pl.ds(0, count, stride=STRIDE), :]
    for s in range(1, 8):
        total += partial[pl.ds(s, count, stride=STRIDE), :]
    out_ref[...] = total


def moments_kernel(
    counts_ref,
    coords_ref,
    masses_ref,
    all_coords,
    all_masses,
    out_ref,
    turned_ref,
    coords,
    masses,
    got,
    send_sem,
    recv_sem,
    px,
    py,
    pz,
    partial,
):
    step = pl.program_id(0)
    stays = pl.num_programs(0) - SWAPS
    space, sub = lax.axis_index("space"), lax.axis_index("sub")
    spaces = lax.axis_size("space")
    partners = (
        (lax.rem(space + spaces // 2, spaces), sub),
        (space + 1 - 2 * lax.rem(space, 2), sub),
        (space, sub + 1 - 2 * lax.rem(sub, 2)),
    )
    column = lax.broadcasted_iota(jnp.int32, (REGION, BLOCK), 0) * BLOCK + lax.broadcasted_iota(
        jnp.int32, (REGION, BLOCK), 1
    )

    def copies(rnd):
        at = pl.ds(rnd * REGION, REGION)
        pairs = ((all_coords.at[:, at, :], got.at[rnd, pl.ds(0, 3)]), (all_masses.at[at, :], got.at[rnd, 3]))
        return [
            pltpu.make_async_remote_copy(
                src_ref=source,
                dst_ref=target,
                send_sem=send_sem.at[2 * rnd + k],
                recv_sem=recv_sem.at[2 * rnd + k],
                device_id=partners[rnd],
                device_id_type=pl.DeviceIdType.MESH,
            )
            for k, (source, target) in enumerate(pairs)
        ]

    @pl.when(step == 0)
    def _():
        barrier = pltpu.get_barrier_semaphore()
        for partner in partners:
            pl.semaphore_signal(barrier, inc=1, device_id=partner, device_id_type=pl.DeviceIdType.MESH)
        pl.semaphore_wait(barrier, SWAPS)
        for rnd in range(SWAPS):
            for copy in copies(rnd):
                copy.start()

    @pl.when(step < stays)
    def _():
        coords[...] = coords_ref[...]
        masses[...] = masses_ref[...]

    for rnd in range(SWAPS):

        @pl.when(step == stays + rnd)
        def _():
            for copy in copies(rnd):
                copy.wait_recv()
            keep = column < counts_ref[rnd]
            for dim in range(3):
                coords[dim] = jnp.where(keep, got[rnd, dim], coords_ref[dim])
            masses[...] = jnp.where(keep, got[rnd, 3], masses_ref[...])

    gather_moments(coords, masses, out_ref, turned_ref, px, py, pz, partial)

    @pl.when(step == stays + SWAPS - 1)
    def _():
        for rnd in range(SWAPS):
            for copy in copies(rnd):
                copy.wait_send()


def moment_scratch(nodes_count):
    return [pltpu.VMEM((ORDER, BLOCK, REGION), jnp.float32) for _ in range(3)] + [
        pltpu.VMEM((STRIDE * nodes_count, REGION), jnp.float32)
    ]


def coefficients_kernel(
    send_ref, sums_ref, leaf_ref, compress_ref, own_ref, got_ref, padded, packed, send_sem, recv_sem
):
    leaves = own_ref.shape[0]
    peers = got_ref.shape[0] // 16
    subs = lax.axis_size("sub")
    me = lax.axis_index("space") * subs + lax.axis_index("sub")
    barrier = pltpu.get_barrier_semaphore()

    def greet(hop, carry):
        peer = lax.rem(me + hop, peers)
        pl.semaphore_signal(
            barrier, inc=1, device_id=(peer // subs, lax.rem(peer, subs)), device_id_type=pl.DeviceIdType.MESH
        )
        return carry

    lax.fori_loop(1, peers, greet, 0)
    onehot = lax.broadcasted_iota(jnp.int32, (leaves, leaf_ref.shape[1]), 0) == leaf_ref[...]
    onehot = jnp.where(onehot, 1.0, 0.0).astype(jnp.bfloat16)
    moved = jnp.dot(
        compress_ref[...], sums_ref[...], precision=lax.Precision.HIGHEST, preferred_element_type=jnp.float32
    )
    both = jnp.concatenate(split_two(moved), axis=0)
    total = lax.dot_general(onehot, both, (((1,), (1,)), ((), ())), preferred_element_type=jnp.float32)
    own = (total + pltpu.roll(total, RANK, 1)).astype(jnp.bfloat16).astype(jnp.float32)
    own_ref[...] = own
    padded[pl.ds(0, 8), :] = jnp.zeros((8, 2 * RANK), jnp.float32)
    padded[pl.ds(8, leaves), :] = own
    padded[pl.ds(8 + leaves, 8), :] = jnp.zeros((8, 2 * RANK), jnp.float32)
    row_of = lax.broadcasted_iota(jnp.int32, (8, 2 * RANK), 0)
    low = lax.broadcasted_iota(jnp.int32, (8, 2 * RANK), 1) < RANK

    def pack(peer):
        line = send_ref.at[pl.ds(peer * 32, 32)]
        halves = []
        for start in (0, 8):
            rows = None
            for j in range(8):
                slot = 2 * (start + j)
                both = jnp.where(low, padded[pl.ds(line[slot], 8), :], padded[pl.ds(line[slot + 1], 8), :])
                rows = both if rows is None else jnp.where(row_of == j, both, rows)
            halves.append(rows)
        return jnp.concatenate(halves, axis=0).astype(jnp.bfloat16)

    def send(hops):
        rows = [lax.rem(me + hop, peers) for hop in hops]
        for peer in rows:
            packed[pl.ds(pl.multiple_of(peer * 16, 16), 16), :] = pack(peer)
        for peer in rows:
            pltpu.make_async_remote_copy(
                src_ref=packed.at[pl.ds(pl.multiple_of(peer * 16, 16), 16), :],
                dst_ref=got_ref.at[mine, :],
                send_sem=send_sem,
                recv_sem=recv_sem,
                device_id=(peer // subs, lax.rem(peer, subs)),
                device_id_type=pl.DeviceIdType.MESH,
            ).start()

    def send_batch(batch, carry):
        send([1 + batch * BATCH + k for k in range(BATCH)])
        return carry

    mine = pl.ds(pl.multiple_of(me * 16, 16), 16)
    got_ref[mine, :] = pack(me)
    pl.semaphore_wait(barrier, peers - 1)
    batches = (peers - 1) // BATCH
    lax.fori_loop(0, batches, send_batch, 0)
    if batches * BATCH < peers - 1:
        send(range(1 + batches * BATCH, peers))
    others = pl.ds(0, (peers - 1) * 16)
    everything = pltpu.make_async_remote_copy(
        src_ref=packed.at[others, :],
        dst_ref=got_ref.at[others, :],
        send_sem=send_sem,
        recv_sem=recv_sem,
        device_id=(lax.axis_index("space"), lax.axis_index("sub")),
        device_id_type=pl.DeviceIdType.MESH,
    )
    everything.wait_send()
    everything.wait_recv()


def translate_kernel(leaves, inter, src_ref, off_ref, own_ref, ghost_ref, kernels_ref, out_ref, tab, iota, held, placed, m2l_ref, sem):
    step = pl.program_id(0)
    last = pl.num_programs(0) - 1
    rows = (tab.shape[0] - 16) // 2
    ghosts = ghost_ref.shape[0]

    @pl.when(step == 0)
    def _():
        width = kernels_ref.shape[1]
        copy = pltpu.make_async_copy(kernels_ref, m2l_ref.at[:, pl.ds(0, width)], sem)
        copy.start()
        m2l_ref[:, pl.ds(width, m2l_ref.shape[1] - width)] = jnp.zeros(
            (m2l_ref.shape[0], m2l_ref.shape[1] - width), jnp.bfloat16
        )
        iota[...] = lax.broadcasted_iota(jnp.int32, iota.shape, 0).astype(jnp.float32).astype(jnp.bfloat16)
        held[...] = jnp.zeros_like(held)
        tab[pl.ds(0, 8), :] = jnp.zeros((8, 128), jnp.float32)
        tab[pl.ds(2 * rows + 8, 8), :] = jnp.zeros((8, 128), jnp.float32)
        low = lax.broadcasted_iota(jnp.int32, (leaves, 128), 1) < 64
        own = own_ref[...]
        tab[pl.ds(8, leaves), :] = jnp.where(low, own, 0.0)
        tab[pl.ds(8 + rows, leaves), :] = jnp.where(low, 0.0, own)
        low = lax.broadcasted_iota(jnp.int32, (ghosts, 128), 1) < 64
        got = ghost_ref[...].astype(jnp.float32)
        turned = pltpu.roll(got, 64, 1)
        tab[pl.ds(8 + leaves, ghosts), :] = jnp.where(low, got, 0.0)
        tab[pl.ds(8 + leaves + ghosts, ghosts), :] = jnp.where(low, turned, 0.0)
        tab[pl.ds(8 + rows + leaves, ghosts), :] = jnp.where(low, 0.0, turned)
        tab[pl.ds(8 + rows + leaves + ghosts, ghosts), :] = jnp.where(low, 0.0, got)
        copy.wait()

    now = lax.rem(step, 2) * (PAIRS * PITCH)
    before = lax.rem(step + 1, 2) * (PAIRS * PITCH)
    lane_of = lax.broadcasted_iota(jnp.int32, (8, 128), 0)

    def collect(cells, slots):
        lines = [src_ref.at[pl.ds(cell * SLOTS, SLOTS)] for cell in cells]
        for pack in range(SLOTS // 16):
            parts = [[] for _ in cells]
            for start in (pack * 16, pack * 16 + 8):
                totals = [None] * len(cells)
                for j in range(min(8, inter - start)):
                    for u, line in enumerate(lines):
                        window = tab[pl.ds(line[start + j], 8), :]
                        totals[u] = window if j == 0 else jnp.where(lane_of == j, window, totals[u])
                for u in range(len(cells)):
                    parts[u].append(totals[u])
            for u, slot in enumerate(slots):
                held[slot, pl.ds(pack * 16, 16), :] = jnp.concatenate(parts[u], axis=0).astype(jnp.bfloat16)

    def pick(cell, rows_of):
        line = jnp.broadcast_to(off_ref[pl.ds(cell, 1), :], (16, 256)).astype(jnp.bfloat16)
        line = jnp.concatenate([line] * (PAIRS // 16), axis=0)
        chosen = jnp.where(iota[...] == line, jnp.bfloat16(1), jnp.bfloat16(0))
        return jnp.dot(chosen[:, :SLOTS], rows_of, preferred_element_type=jnp.float32)

    def contract(tile, count):
        pieces = []
        for t in range(2 * count):
            at = before + (2 * tile + t) * PITCH
            pieces.append(placed[pl.ds(at, GROUP), :].astype(jnp.bfloat16))
        both = jnp.concatenate(pieces, axis=1)
        kern = m2l_ref[:, pl.ds(pl.multiple_of(tile * 256, 256), 256 * count)]
        return lax.dot_general(both, kern, (((1,), (1,)), ((), ())), preferred_element_type=jnp.float32)

    out_ref[...] = jnp.zeros_like(out_ref)

    @pl.when(step < last)
    def _():
        def body(it, carry):
            cell = UNROLL * it
            part = contract(cell, UNROLL)
            olds = [held[u] for u in range(UNROLL)]
            results = []
            for u in range(UNROLL):
                back = jnp.where(it == 0, GROUP - UNROLL, cell - UNROLL) + u
                results.append((back, pick(back, olds[u])))
            collect([cell + u for u in range(UNROLL)], list(range(UNROLL)))
            for back, result in results:
                placed[pl.ds(now + back, PAIRS, stride=PITCH), :] = result
            out_ref[...] += part
            return carry
        lax.fori_loop(0, GROUP // UNROLL, body, 0)
        for u in range(UNROLL):
            back = GROUP - UNROLL + u
            placed[pl.ds(now + back, PAIRS, stride=PITCH), :] = pick(back, held[u])

    @pl.when(step == last)
    def _():
        def body(it, carry):
            out_ref[...] += contract(it * UNROLL, UNROLL)
            return carry
        lax.fori_loop(0, GROUP // UNROLL, body, 0)


def translate(own, ghost, sources, offsets, m2l_kernels):
    leaves, inter = sources.shape
    ghosts = ghost.shape[0]
    rows = leaves + 2 * ghosts
    remote = sources - leaves
    row = jnp.where(remote < 0, sources, leaves + lax.shift_right_arithmetic(remote, 1) + (remote & 1) * ghosts)
    row = row + (offsets & 1) * rows
    row = row + 8 - jnp.arange(inter, dtype=jnp.int32)[None, :] % 8
    row = jnp.pad(row, ((0, 0), (0, SLOTS - inter))).reshape(-1)
    pair = jnp.pad((offsets >> 1).astype(jnp.float32), ((0, 0), (0, 256 - inter)), constant_values=-1.0)
    steps = leaves // GROUP
    return pl.pallas_call(
        functools.partial(translate_kernel, leaves, inter),
        grid=(steps + 1,),
        in_specs=[
            pl.BlockSpec((GROUP * SLOTS,), lambda i: (jnp.minimum(i, steps - 1),), memory_space=pltpu.SMEM),
            pl.BlockSpec((GROUP, 256), lambda i: (jnp.minimum(i, steps - 1), 0)),
            pl.BlockSpec(own.shape, lambda i: (0, 0)),
            pl.BlockSpec(ghost.shape, lambda i: (0, 0)),
            pl.BlockSpec(memory_space=pl.ANY),
        ],
        out_specs=pl.BlockSpec((GROUP, 64), lambda i: (jnp.maximum(i - 1, 0), 0)),
        out_shape=jax.ShapeDtypeStruct((leaves, 64), jnp.float32),
        scratch_shapes=[
            pltpu.VMEM((2 * rows + 16, 128), jnp.float32),
            pltpu.VMEM((PAIRS, 256), jnp.bfloat16),
            pltpu.VMEM((UNROLL, SLOTS, 128), jnp.bfloat16),
            pltpu.VMEM((2 * PAIRS * PITCH, 128), jnp.float32),
            pltpu.VMEM((RANK, PAIRS * 128), jnp.bfloat16),
            pltpu.SemaphoreType.DMA,
        ],
        compiler_params=params(),
    )(row, pair, own, ghost, m2l_kernels)


def evaluate_kernel(turned_ref, leaf_ref, local_ref, expand_ref, out_ref, nodes, result):
    step = pl.program_id(0)
    leaves = local_ref.shape[0]

    @pl.when(step == 0)
    def _():
        local = jnp.concatenate([part.astype(jnp.float32) for part in split_two(local_ref[...])], axis=1)
        local = local.T.astype(jnp.bfloat16)
        large, small = split_two(expand_ref[...])
        expands = jnp.concatenate([large, large, small], axis=1)
        width = 2 * REGION
        for pair in range(nodes.shape[0] // 2):
            ids = leaf_ref[:, pl.ds(pair * width, width)]
            onehot = lax.broadcasted_iota(jnp.int32, (leaves, width), 0) == ids
            onehot = jnp.where(onehot, 1.0, 0.0).astype(jnp.bfloat16)
            picked = jnp.dot(local, onehot, preferred_element_type=jnp.float32).astype(jnp.bfloat16)
            terms = jnp.concatenate([picked, picked[:RANK]], axis=0)
            values = jnp.dot(expands, terms, preferred_element_type=jnp.float32)
            nodes[2 * pair] = values[:, :REGION]
            nodes[2 * pair + 1] = values[:, REGION:]

    def chunk(v, carry):
        at = pl.ds(pl.multiple_of(v * 16, 16), 16)
        px, py, pz = (chebyshev(turned_ref[dim, at, :]) for dim in range(3))
        value = None
        for i in range(ORDER):
            middle = None
            for j in range(ORDER):
                first = (i * ORDER + j) * ORDER
                inner = nodes[step, pl.ds(first + 1, 1), :] * pz[0] + nodes[step, pl.ds(first, 1), :]
                for k in range(2, ORDER):
                    inner += nodes[step, pl.ds(first + k, 1), :] * pz[k - 1]
                middle = inner if j == 0 else middle + inner * py[j - 1]
            value = middle if i == 0 else value + middle * px[i - 1]
        result[at, :] = value
        return carry

    lax.fori_loop(0, BLOCK // 16, chunk, 0)
    out_ref[...] = result[...].T


def on_device(
    coords,
    masses,
    swap_counts,
    leaf_of_block,
    let_send,
    inter_source,
    inter_offset,
    compress,
    m2l_kernels,
    expand,
):
    nodes_count = compress.shape[0]
    leaves = inter_source.shape[0]
    local_bodies = coords.shape[1]
    blocks = local_bodies // BLOCK
    regions = blocks // REGION
    peers, per_peer = let_send.shape[1:]
    coords = coords.reshape(3, blocks, BLOCK)
    masses = masses.reshape(blocks, BLOCK)
    hbm = pl.BlockSpec(memory_space=pl.ANY)
    coords_block, masses_block = (3, REGION, BLOCK), (REGION, BLOCK)

    def region_of(g):
        return lax.rem(g + SWAPS, regions)

    sums, turned = pl.pallas_call(
        moments_kernel,
        grid=(regions,),
        in_specs=[
            pl.BlockSpec(memory_space=pltpu.SMEM),
            pl.BlockSpec(coords_block, lambda g: (0, region_of(g), 0)),
            pl.BlockSpec(masses_block, lambda g: (region_of(g), 0)),
            hbm,
            hbm,
        ],
        out_specs=[
            pl.BlockSpec((nodes_count, REGION), lambda g: (0, region_of(g))),
            pl.BlockSpec((3, BLOCK, REGION), lambda g: (0, 0, region_of(g))),
        ],
        out_shape=[
            jax.ShapeDtypeStruct((nodes_count, blocks), jnp.float32),
            jax.ShapeDtypeStruct((3, BLOCK, blocks), jnp.float32),
        ],
        scratch_shapes=[
            pltpu.VMEM(coords_block, jnp.float32),
            pltpu.VMEM(masses_block, jnp.float32),
            pltpu.VMEM((SWAPS, 4, REGION, BLOCK), jnp.float32),
            pltpu.SemaphoreType.DMA((2 * SWAPS,)),
            pltpu.SemaphoreType.DMA((2 * SWAPS,)),
        ]
        + moment_scratch(nodes_count),
        compiler_params=params(collective_id=1, has_side_effects=True),
    )(swap_counts.reshape(SWAPS), coords, masses, coords, masses)
    basis = node_basis()
    exact = functools.partial(jnp.dot, precision=lax.Precision.HIGHEST, preferred_element_type=jnp.float32)
    compress_polys = exact(compress.T, basis)
    expand_polys = exact(basis.T, expand.T)
    leaf_row = leaf_of_block.reshape(1, blocks)
    send = let_send.reshape(peers, per_peer) + 8 - (jnp.arange(per_peer, dtype=jnp.int32)[None, :] // 2) % 8
    vmem = pl.BlockSpec(memory_space=pltpu.VMEM)
    own, incoming = pl.pallas_call(
        coefficients_kernel,
        in_specs=[pl.BlockSpec(memory_space=pltpu.SMEM), vmem, vmem, vmem],
        out_specs=[vmem, vmem],
        out_shape=[
            jax.ShapeDtypeStruct((leaves, 2 * RANK), jnp.float32),
            jax.ShapeDtypeStruct((peers * per_peer // 2, 2 * RANK), jnp.bfloat16),
        ],
        scratch_shapes=[
            pltpu.VMEM((leaves + 16, 2 * RANK), jnp.float32),
            pltpu.VMEM((peers * per_peer // 2, 2 * RANK), jnp.bfloat16),
            pltpu.SemaphoreType.DMA,
            pltpu.SemaphoreType.DMA,
        ],
        compiler_params=params(collective_id=0, has_side_effects=True),
    )(send.reshape(-1), sums, leaf_row, compress_polys)
    local = translate(own, incoming, inter_source, inter_offset, m2l_kernels)
    values = pl.pallas_call(
        evaluate_kernel,
        grid=(regions,),
        in_specs=[
            pl.BlockSpec((3, BLOCK, REGION), lambda g: (0, 0, g)),
            pl.BlockSpec((1, blocks), lambda g: (0, 0)),
            pl.BlockSpec((leaves, RANK), lambda g: (0, 0)),
            pl.BlockSpec((nodes_count, RANK), lambda g: (0, 0)),
        ],
        out_specs=pl.BlockSpec((REGION, BLOCK), lambda g: (g, 0)),
        out_shape=jax.ShapeDtypeStruct((blocks, BLOCK), jnp.float32),
        scratch_shapes=[
            pltpu.VMEM((regions, nodes_count, REGION), jnp.float32),
            pltpu.VMEM((BLOCK, REGION), jnp.float32),
        ],
        compiler_params=params(),
    )(turned, leaf_row, local, expand_polys)
    return values.reshape(local_bodies)


def solution(mesh):
    return jax.shard_map(
        on_device,
        mesh=mesh,
        in_specs=(
            P(None, ("space", "sub")),
            P(("space", "sub")),
            P(("space", "sub"), None),
            P(("space", "sub")),
            P(("space", "sub"), None, None),
            P(("space", "sub"), None),
            P(("space", "sub"), None),
            P(),
            P(),
            P(),
        ),
        out_specs=P(("space", "sub")),
        check_vma=False,
    )
```

```python
import functools

import jax
import jax.numpy as jnp
import numpy as np
from jax import lax
from jax.experimental import pallas as pl
from jax.experimental.pallas import tpu as pltpu
from jax.sharding import PartitionSpec as P

ORDER = 6
RANK = 64
BLOCK = 128
REGION = 128
SWAPS = 3
GROUP = 80
SLOTS = 192
PAIRS = 160
PITCH = 81
UNROLL = 8
STRIDE = 9
BATCH = 4


def params(**more):
    return pltpu.CompilerParams(vmem_limit_bytes=56 << 20, **more)


def chebyshev(points):
    twice = 2.0 * points
    polys = [points, twice * points - 1.0]
    for _ in range(ORDER - 3):
        polys.append(twice * polys[-1] - polys[-2])
    return polys


def node_basis():
    single = np.zeros((ORDER, ORDER))
    for j in range(ORDER):
        for k in range(ORDER):
            single[j, k] = np.cos(k * (2 * j + 1) * np.pi / (2 * ORDER)) * (1.0 if k == 0 else 2.0) / ORDER
    return np.kron(np.kron(single, single), single).astype(np.float32)


def split_two(values):
    first = values.astype(jnp.bfloat16)
    return first, (values - first.astype(jnp.float32)).astype(jnp.bfloat16)


def gather_moments(coords, masses, out_ref, turned_ref, px, py, pz, partial):
    mass = masses[...].T
    px[0] = mass
    for dim, scratch in enumerate((px, py, pz)):
        points = coords[dim].T
        turned_ref[dim] = points
        for k, poly in enumerate(chebyshev(points)):
            scratch[k + 1] = poly * mass if dim == 0 else poly

    def along(i, carry):
        def chunk(v, sums):
            at = pl.ds(pl.multiple_of(v * 8, 8), 8)
            left = px[i, at, :]
            inner = [pz[k, at, :] for k in range(1, ORDER)]
            new = []
            for j in range(ORDER):
                pair = left if j == 0 else left * py[j, at, :]
                new.append(sums[j * ORDER] + pair)
                for k in range(1, ORDER):
                    new.append(sums[j * ORDER + k] + pair * inner[k - 1])
            return tuple(new)

        zero = jnp.zeros((8, REGION), jnp.float32)
        sums = lax.fori_loop(0, BLOCK // 8, chunk, (zero,) * (ORDER * ORDER), unroll=4)
        for n in range(ORDER * ORDER):
            partial[pl.ds((i * ORDER * ORDER + n) * STRIDE, 8), :] = sums[n]
        return carry

    lax.fori_loop(0, ORDER, along, 0)
    count = out_ref.shape[0]
    total = partial[pl.ds(0, count, stride=STRIDE), :]
    for s in range(1, 8):
        total += partial[pl.ds(s, count, stride=STRIDE), :]
    out_ref[...] = total


def moments_kernel(
    counts_ref,
    coords_ref,
    masses_ref,
    all_coords,
    all_masses,
    out_ref,
    turned_ref,
    coords,
    masses,
    got,
    send_sem,
    recv_sem,
    px,
    py,
    pz,
    partial,
):
    step = pl.program_id(0)
    stays = pl.num_programs(0) - SWAPS
    space, sub = lax.axis_index("space"), lax.axis_index("sub")
    spaces = lax.axis_size("space")
    partners = (
        (lax.rem(space + spaces // 2, spaces), sub),
        (space + 1 - 2 * lax.rem(space, 2), sub),
        (space, sub + 1 - 2 * lax.rem(sub, 2)),
    )
    column = lax.broadcasted_iota(jnp.int32, (REGION, BLOCK), 0) * BLOCK + lax.broadcasted_iota(
        jnp.int32, (REGION, BLOCK), 1
    )

    def copies(rnd):
        at = pl.ds(rnd * REGION, REGION)
        pairs = ((all_coords.at[:, at, :], got.at[rnd, pl.ds(0, 3)]), (all_masses.at[at, :], got.at[rnd, 3]))
        return [
            pltpu.make_async_remote_copy(
                src_ref=source,
                dst_ref=target,
                send_sem=send_sem.at[2 * rnd + k],
                recv_sem=recv_sem.at[2 * rnd + k],
                device_id=partners[rnd],
                device_id_type=pl.DeviceIdType.MESH,
            )
            for k, (source, target) in enumerate(pairs)
        ]

    @pl.when(step == 0)
    def _():
        barrier = pltpu.get_barrier_semaphore()
        for partner in partners:
            pl.semaphore_signal(barrier, inc=1, device_id=partner, device_id_type=pl.DeviceIdType.MESH)
        pl.semaphore_wait(barrier, SWAPS)
        for rnd in range(SWAPS):
            for copy in copies(rnd):
                copy.start()

    @pl.when(step < stays)
    def _():
        coords[...] = coords_ref[...]
        masses[...] = masses_ref[...]

    for rnd in range(SWAPS):

        @pl.when(step == stays + rnd)
        def _():
            for copy in copies(rnd):
                copy.wait_recv()
            keep = column < counts_ref[rnd]
            for dim in range(3):
                coords[dim] = jnp.where(keep, got[rnd, dim], coords_ref[dim])
            masses[...] = jnp.where(keep, got[rnd, 3], masses_ref[...])

    gather_moments(coords, masses, out_ref, turned_ref, px, py, pz, partial)

    @pl.when(step == stays + SWAPS - 1)
    def _():
        for rnd in range(SWAPS):
            for copy in copies(rnd):
                copy.wait_send()


def moment_scratch(nodes_count):
    return [pltpu.VMEM((ORDER, BLOCK, REGION), jnp.float32) for _ in range(3)] + [
        pltpu.VMEM((STRIDE * nodes_count, REGION), jnp.float32)
    ]


def coefficients_kernel(
    send_ref, sums_ref, leaf_ref, compress_ref, own_ref, got_ref, padded, packed, send_sem, recv_sem
):
    leaves = own_ref.shape[0]
    peers = got_ref.shape[0] // 16
    subs = lax.axis_size("sub")
    me = lax.axis_index("space") * subs + lax.axis_index("sub")
    barrier = pltpu.get_barrier_semaphore()

    def greet(hop, carry):
        peer = lax.rem(me + hop, peers)
        pl.semaphore_signal(
            barrier, inc=1, device_id=(peer // subs, lax.rem(peer, subs)), device_id_type=pl.DeviceIdType.MESH
        )
        return carry

    lax.fori_loop(1, peers, greet, 0)
    onehot = lax.broadcasted_iota(jnp.int32, (leaves, leaf_ref.shape[1]), 0) == leaf_ref[...]
    onehot = jnp.where(onehot, 1.0, 0.0).astype(jnp.bfloat16)
    moved = jnp.dot(
        compress_ref[...], sums_ref[...], precision=lax.Precision.HIGHEST, preferred_element_type=jnp.float32
    )
    both = jnp.concatenate(split_two(moved), axis=0)
    total = lax.dot_general(onehot, both, (((1,), (1,)), ((), ())), preferred_element_type=jnp.float32)
    own = (total + pltpu.roll(total, RANK, 1)).astype(jnp.bfloat16).astype(jnp.float32)
    own_ref[...] = own
    padded[pl.ds(0, 8), :] = jnp.zeros((8, 2 * RANK), jnp.float32)
    padded[pl.ds(8, leaves), :] = own
    padded[pl.ds(8 + leaves, 8), :] = jnp.zeros((8, 2 * RANK), jnp.float32)
    row_of = lax.broadcasted_iota(jnp.int32, (8, 2 * RANK), 0)
    low = lax.broadcasted_iota(jnp.int32, (8, 2 * RANK), 1) < RANK

    def pack(peer):
        line = send_ref.at[pl.ds(peer * 32, 32)]
        halves = []
        for start in (0, 8):
            rows = None
            for j in range(8):
                slot = 2 * (start + j)
                both = jnp.where(low, padded[pl.ds(line[slot], 8), :], padded[pl.ds(line[slot + 1], 8), :])
                rows = both if rows is None else jnp.where(row_of == j, both, rows)
            halves.append(rows)
        return jnp.concatenate(halves, axis=0).astype(jnp.bfloat16)

    def send(hops):
        rows = [lax.rem(me + hop, peers) for hop in hops]
        for peer in rows:
            packed[pl.ds(pl.multiple_of(peer * 16, 16), 16), :] = pack(peer)
        for peer in rows:
            pltpu.make_async_remote_copy(
                src_ref=packed.at[pl.ds(pl.multiple_of(peer * 16, 16), 16), :],
                dst_ref=got_ref.at[mine, :],
                send_sem=send_sem,
                recv_sem=recv_sem,
                device_id=(peer // subs, lax.rem(peer, subs)),
                device_id_type=pl.DeviceIdType.MESH,
            ).start()

    def send_batch(batch, carry):
        send([1 + batch * BATCH + k for k in range(BATCH)])
        return carry

    mine = pl.ds(pl.multiple_of(me * 16, 16), 16)
    got_ref[mine, :] = pack(me)
    pl.semaphore_wait(barrier, peers - 1)
    batches = (peers - 1) // BATCH
    lax.fori_loop(0, batches, send_batch, 0)
    if batches * BATCH < peers - 1:
        send(range(1 + batches * BATCH, peers))
    others = pl.ds(0, (peers - 1) * 16)
    everything = pltpu.make_async_remote_copy(
        src_ref=packed.at[others, :],
        dst_ref=got_ref.at[others, :],
        send_sem=send_sem,
        recv_sem=recv_sem,
        device_id=(lax.axis_index("space"), lax.axis_index("sub")),
        device_id_type=pl.DeviceIdType.MESH,
    )
    everything.wait_send()
    everything.wait_recv()


def translate_kernel(leaves, inter, src_ref, off_ref, own_ref, ghost_ref, kernels_ref, out_ref, tab, iota, held, placed, m2l_ref, sem):
    step = pl.program_id(0)
    last = pl.num_programs(0) - 1
    rows = (tab.shape[0] - 16) // 2
    ghosts = ghost_ref.shape[0]

    @pl.when(step == 0)
    def _():
        width = kernels_ref.shape[1]
        copy = pltpu.make_async_copy(kernels_ref, m2l_ref.at[:, pl.ds(0, width)], sem)
        copy.start()
        m2l_ref[:, pl.ds(width, m2l_ref.shape[1] - width)] = jnp.zeros(
            (m2l_ref.shape[0], m2l_ref.shape[1] - width), jnp.bfloat16
        )
        iota[...] = lax.broadcasted_iota(jnp.int32, iota.shape, 0).astype(jnp.float32).astype(jnp.bfloat16)
        held[...] = jnp.zeros_like(held)
        tab[pl.ds(0, 8), :] = jnp.zeros((8, 128), jnp.float32)
        tab[pl.ds(2 * rows + 8, 8), :] = jnp.zeros((8, 128), jnp.float32)
        low = lax.broadcasted_iota(jnp.int32, (leaves, 128), 1) < 64
        own = own_ref[...]
        tab[pl.ds(8, leaves), :] = jnp.where(low, own, 0.0)
        tab[pl.ds(8 + rows, leaves), :] = jnp.where(low, 0.0, own)
        low = lax.broadcasted_iota(jnp.int32, (ghosts, 128), 1) < 64
        got = ghost_ref[...].astype(jnp.float32)
        turned = pltpu.roll(got, 64, 1)
        tab[pl.ds(8 + leaves, ghosts), :] = jnp.where(low, got, 0.0)
        tab[pl.ds(8 + leaves + ghosts, ghosts), :] = jnp.where(low, turned, 0.0)
        tab[pl.ds(8 + rows + leaves, ghosts), :] = jnp.where(low, 0.0, turned)
        tab[pl.ds(8 + rows + leaves + ghosts, ghosts), :] = jnp.where(low, 0.0, got)
        copy.wait()

    now = lax.rem(step, 2) * (PAIRS * PITCH)
    before = lax.rem(step + 1, 2) * (PAIRS * PITCH)
    lane_of = lax.broadcasted_iota(jnp.int32, (8, 128), 0)

    def collect(cells, slots):
        lines = [src_ref.at[pl.ds(cell * SLOTS, SLOTS)] for cell in cells]
        for pack in range(SLOTS // 16):
            parts = [[] for _ in cells]
            for start in (pack * 16, pack * 16 + 8):
                totals = [None] * len(cells)
                for j in range(min(8, inter - start)):
                    for u, line in enumerate(lines):
                        window = tab[pl.ds(line[start + j], 8), :]
                        totals[u] = window if j == 0 else jnp.where(lane_of == j, window, totals[u])
                for u in range(len(cells)):
                    parts[u].append(totals[u])
            for u, slot in enumerate(slots):
                held[slot, pl.ds(pack * 16, 16), :] = jnp.concatenate(parts[u], axis=0).astype(jnp.bfloat16)

    def pick(cell, rows_of):
        line = jnp.broadcast_to(off_ref[pl.ds(cell, 1), :], (16, 256)).astype(jnp.bfloat16)
        line = jnp.concatenate([line] * (PAIRS // 16), axis=0)
        chosen = jnp.where(iota[...] == line, jnp.bfloat16(1), jnp.bfloat16(0))
        return jnp.dot(chosen[:, :SLOTS], rows_of, preferred_element_type=jnp.float32)

    def contract(tile, count):
        pieces = []
        for t in range(2 * count):
            at = before + (2 * tile + t) * PITCH
            pieces.append(placed[pl.ds(at, GROUP), :].astype(jnp.bfloat16))
        both = jnp.concatenate(pieces, axis=1)
        kern = m2l_ref[:, pl.ds(pl.multiple_of(tile * 256, 256), 256 * count)]
        return lax.dot_general(both, kern, (((1,), (1,)), ((), ())), preferred_element_type=jnp.float32)

    out_ref[...] = jnp.zeros_like(out_ref)

    @pl.when(step < last)
    def _():
        def body(it, carry):
            cell = UNROLL * it
            part = contract(cell, UNROLL)
            olds = [held[u] for u in range(UNROLL)]
            results = []
            for u in range(UNROLL):
                back = jnp.where(it == 0, GROUP - UNROLL, cell - UNROLL) + u
                results.append((back, pick(back, olds[u])))
            collect([cell + u for u in range(UNROLL)], list(range(UNROLL)))
            for back, result in results:
                placed[pl.ds(now + back, PAIRS, stride=PITCH), :] = result
            out_ref[...] += part
            return carry
        lax.fori_loop(0, GROUP // UNROLL, body, 0)
        for u in range(UNROLL):
            back = GROUP - UNROLL + u
            placed[pl.ds(now + back, PAIRS, stride=PITCH), :] = pick(back, held[u])

    @pl.when(step == last)
    def _():
        def body(it, carry):
            out_ref[...] += contract(it * UNROLL, UNROLL)
            return carry
        lax.fori_loop(0, GROUP // UNROLL, body, 0)


def translate(own, ghost, sources, offsets, m2l_kernels):
    leaves, inter = sources.shape
    ghosts = ghost.shape[0]
    rows = leaves + 2 * ghosts
    remote = sources - leaves
    row = jnp.where(remote < 0, sources, leaves + lax.shift_right_arithmetic(remote, 1) + (remote & 1) * ghosts)
    row = row + (offsets & 1) * rows
    row = row + 8 - jnp.arange(inter, dtype=jnp.int32)[None, :] % 8
    row = jnp.pad(row, ((0, 0), (0, SLOTS - inter))).reshape(-1)
    pair = jnp.pad((offsets >> 1).astype(jnp.float32), ((0, 0), (0, 256 - inter)), constant_values=-1.0)
    steps = leaves // GROUP
    return pl.pallas_call(
        functools.partial(translate_kernel, leaves, inter),
        grid=(steps + 1,),
        in_specs=[
            pl.BlockSpec((GROUP * SLOTS,), lambda i: (jnp.minimum(i, steps - 1),), memory_space=pltpu.SMEM),
            pl.BlockSpec((GROUP, 256), lambda i: (jnp.minimum(i, steps - 1), 0)),
            pl.BlockSpec(own.shape, lambda i: (0, 0)),
            pl.BlockSpec(ghost.shape, lambda i: (0, 0)),
            pl.BlockSpec(memory_space=pl.ANY),
        ],
        out_specs=pl.BlockSpec((GROUP, 64), lambda i: (jnp.maximum(i - 1, 0), 0)),
        out_shape=jax.ShapeDtypeStruct((leaves, 64), jnp.float32),
        scratch_shapes=[
            pltpu.VMEM((2 * rows + 16, 128), jnp.float32),
            pltpu.VMEM((PAIRS, 256), jnp.bfloat16),
            pltpu.VMEM((UNROLL, SLOTS, 128), jnp.bfloat16),
            pltpu.VMEM((2 * PAIRS * PITCH, 128), jnp.float32),
            pltpu.VMEM((RANK, PAIRS * 128), jnp.bfloat16),
            pltpu.SemaphoreType.DMA,
        ],
        compiler_params=params(),
    )(row, pair, own, ghost, m2l_kernels)


def evaluate_kernel(turned_ref, leaf_ref, local_ref, expand_ref, out_ref, nodes, result):
    step = pl.program_id(0)
    leaves = local_ref.shape[0]

    @pl.when(step == 0)
    def _():
        local = jnp.concatenate([part.astype(jnp.float32) for part in split_two(local_ref[...])], axis=1)
        local = local.T.astype(jnp.bfloat16)
        large, small = split_two(expand_ref[...])
        expands = jnp.concatenate([large, large, small], axis=1)
        width = 2 * REGION
        for pair in range(nodes.shape[0] // 2):
            ids = leaf_ref[:, pl.ds(pair * width, width)]
            onehot = lax.broadcasted_iota(jnp.int32, (leaves, width), 0) == ids
            onehot = jnp.where(onehot, 1.0, 0.0).astype(jnp.bfloat16)
            picked = jnp.dot(local, onehot, preferred_element_type=jnp.float32).astype(jnp.bfloat16)
            terms = jnp.concatenate([picked, picked[:RANK]], axis=0)
            values = jnp.dot(expands, terms, preferred_element_type=jnp.float32)
            nodes[2 * pair] = values[:, :REGION]
            nodes[2 * pair + 1] = values[:, REGION:]

    for half in range(2):
        lanes = slice(half * REGION, (half + 1) * REGION)
        region = 2 * step + half

        def chunk(v, carry):
            at = pl.ds(pl.multiple_of(v * 16, 16), 16)
            px, py, pz = (chebyshev(turned_ref[dim, at, lanes]) for dim in range(3))
            value = None
            for i in range(ORDER):
                middle = None
                for j in range(ORDER):
                    first = (i * ORDER + j) * ORDER
                    inner = nodes[region, pl.ds(first + 1, 1), :] * pz[0] + nodes[region, pl.ds(first, 1), :]
                    for k in range(2, ORDER):
                        inner += nodes[region, pl.ds(first + k, 1), :] * pz[k - 1]
                    middle = inner if j == 0 else middle + inner * py[j - 1]
                value = middle if i == 0 else value + middle * px[i - 1]
            result[at, :] = value
            return carry

        lax.fori_loop(0, BLOCK // 16, chunk, 0)
        out_ref[lanes, :] = result[...].T


def on_device(
    coords,
    masses,
    swap_counts,
    leaf_of_block,
    let_send,
    inter_source,
    inter_offset,
    compress,
    m2l_kernels,
    expand,
):
    nodes_count = compress.shape[0]
    leaves = inter_source.shape[0]
    local_bodies = coords.shape[1]
    blocks = local_bodies // BLOCK
    regions = blocks // REGION
    peers, per_peer = let_send.shape[1:]
    coords = coords.reshape(3, blocks, BLOCK)
    masses = masses.reshape(blocks, BLOCK)
    hbm = pl.BlockSpec(memory_space=pl.ANY)
    coords_block, masses_block = (3, REGION, BLOCK), (REGION, BLOCK)

    def region_of(g):
        return lax.rem(g + SWAPS, regions)

    sums, turned = pl.pallas_call(
        moments_kernel,
        grid=(regions,),
        in_specs=[
            pl.BlockSpec(memory_space=pltpu.SMEM),
            pl.BlockSpec(coords_block, lambda g: (0, region_of(g), 0)),
            pl.BlockSpec(masses_block, lambda g: (region_of(g), 0)),
            hbm,
            hbm,
        ],
        out_specs=[
            pl.BlockSpec((nodes_count, REGION), lambda g: (0, region_of(g))),
            pl.BlockSpec((3, BLOCK, REGION), lambda g: (0, 0, region_of(g))),
        ],
        out_shape=[
            jax.ShapeDtypeStruct((nodes_count, blocks), jnp.float32),
            jax.ShapeDtypeStruct((3, BLOCK, blocks), jnp.float32),
        ],
        scratch_shapes=[
            pltpu.VMEM(coords_block, jnp.float32),
            pltpu.VMEM(masses_block, jnp.float32),
            pltpu.VMEM((SWAPS, 4, REGION, BLOCK), jnp.float32),
            pltpu.SemaphoreType.DMA((2 * SWAPS,)),
            pltpu.SemaphoreType.DMA((2 * SWAPS,)),
        ]
        + moment_scratch(nodes_count),
        compiler_params=params(collective_id=1, has_side_effects=True),
    )(swap_counts.reshape(SWAPS), coords, masses, coords, masses)
    basis = node_basis()
    exact = functools.partial(jnp.dot, precision=lax.Precision.HIGHEST, preferred_element_type=jnp.float32)
    compress_polys = exact(compress.T, basis)
    expand_polys = exact(basis.T, expand.T)
    leaf_row = leaf_of_block.reshape(1, blocks)
    send = let_send.reshape(peers, per_peer) + 8 - (jnp.arange(per_peer, dtype=jnp.int32)[None, :] // 2) % 8
    vmem = pl.BlockSpec(memory_space=pltpu.VMEM)
    own, incoming = pl.pallas_call(
        coefficients_kernel,
        in_specs=[pl.BlockSpec(memory_space=pltpu.SMEM), vmem, vmem, vmem],
        out_specs=[vmem, vmem],
        out_shape=[
            jax.ShapeDtypeStruct((leaves, 2 * RANK), jnp.float32),
            jax.ShapeDtypeStruct((peers * per_peer // 2, 2 * RANK), jnp.bfloat16),
        ],
        scratch_shapes=[
            pltpu.VMEM((leaves + 16, 2 * RANK), jnp.float32),
            pltpu.VMEM((peers * per_peer // 2, 2 * RANK), jnp.bfloat16),
            pltpu.SemaphoreType.DMA,
            pltpu.SemaphoreType.DMA,
        ],
        compiler_params=params(collective_id=0, has_side_effects=True),
    )(send.reshape(-1), sums, leaf_row, compress_polys)
    local = translate(own, incoming, inter_source, inter_offset, m2l_kernels)
    values = pl.pallas_call(
        evaluate_kernel,
        grid=(regions // 2,),
        in_specs=[
            pl.BlockSpec((3, BLOCK, 2 * REGION), lambda g: (0, 0, g)),
            pl.BlockSpec((1, blocks), lambda g: (0, 0)),
            pl.BlockSpec((leaves, RANK), lambda g: (0, 0)),
            pl.BlockSpec((nodes_count, RANK), lambda g: (0, 0)),
        ],
        out_specs=pl.BlockSpec((2 * REGION, BLOCK), lambda g: (g, 0)),
        out_shape=jax.ShapeDtypeStruct((blocks, BLOCK), jnp.float32),
        scratch_shapes=[
            pltpu.VMEM((regions, nodes_count, REGION), jnp.float32),
            pltpu.VMEM((BLOCK, REGION), jnp.float32),
        ],
        compiler_params=params(),
    )(turned, leaf_row, local, expand_polys)
    return values.reshape(local_bodies)


def solution(mesh):
    return jax.shard_map(
        on_device,
        mesh=mesh,
        in_specs=(
            P(None, ("space", "sub")),
            P(("space", "sub")),
            P(("space", "sub"), None),
            P(("space", "sub")),
            P(("space", "sub"), None, None),
            P(("space", "sub"), None),
            P(("space", "sub"), None),
            P(),
            P(),
            P(),
        ),
        out_specs=P(("space", "sub")),
        check_vma=False,
    )
```
